32 devices in a mesh: dp: 16 (over z, y, x), seq: 2 (over core).
Axes of the slice: x: 2, y: 2, z: 4, core: 2. Of those that a mesh axis runs over, the one named last changes fastest.
Arguments:
- inputs: bfloat16 [8192, 1280], P(('dp', 'seq')), may hold values from -6 to 6
- lengths: int32 [16], P('dp'), may hold values from 257 to 512, as said below
- cotangent: bfloat16 [8192, 1280], P(('dp', 'seq')), may hold values from -6 to 6
- norm1_gain: bfloat16 [1280], P('dp'), may hold values from 0.25 to 1.75
- norm1_shift: bfloat16 [1280], P('dp'), may hold values from -4 to 4
- w_query: bfloat16 [1280, 1280], P('dp'), may hold values from -0.15625 to 0.15625
- b_query: bfloat16 [1280], P('dp'), may hold values from -4 to 4
- w_key: bfloat16 [1280, 1280], P('dp'), may hold values from -0.15625 to 0.15625
- w_value: bfloat16 [1280, 1280], P('dp'), may hold values from -0.15625 to 0.15625
- b_value: bfloat16 [1280], P('dp'), may hold values from -0.75 to 0.75
- w_output: bfloat16 [1280, 1280], P('dp'), may hold values from -3 to 3
- b_output: bfloat16 [1280], P('dp'), may hold values from -4 to 4
- norm2_gain: bfloat16 [1280], P('dp'), may hold values from 0.25 to 1.75
- norm2_shift: bfloat16 [1280], P('dp'), may hold values from -4 to 4
- w_up: bfloat16 [1280, 5120], P('dp'), may hold values from -0.15625 to 0.15625
- b_up: bfloat16 [5120], P('dp'), may hold values from -4 to 4
- w_down: bfloat16 [5120, 1280], P('dp'), may hold values from -0.078125 to 0.078125
- b_down: bfloat16 [1280], P('dp'), may hold values from -4 to 4
Outputs:
- output: bfloat16 [8192, 1280], P(('dp', 'seq'))
- input_grad: float32 [8192, 1280], P(('dp', 'seq'))
- grad_norm1_gain: float32 [1280], P(('dp', 'seq'))
- grad_norm1_shift: float32 [1280], P(('dp', 'seq'))
- grad_w_query: float32 [1280, 1280], P(('dp', 'seq'))
- grad_b_query: float32 [1280], P(('dp', 'seq'))
- grad_w_key: float32 [1280, 1280], P(('dp', 'seq'))
- grad_w_value: float32 [1280, 1280], P(('dp', 'seq'))
- grad_b_value: float32 [1280], P(('dp', 'seq'))
- grad_w_output: float32 [1280, 1280], P(('dp', 'seq'))
- grad_b_output: float32 [1280], P(('dp', 'seq'))
- grad_norm2_gain: float32 [1280], P(('dp', 'seq'))
- grad_norm2_shift: float32 [1280], P(('dp', 'seq'))
- grad_w_up: float32 [1280, 5120], P(('dp', 'seq'))
- grad_b_up: float32 [5120], P(('dp', 'seq'))
- grad_w_down: float32 [5120, 1280], P(('dp', 'seq'))
- grad_b_down: float32 [1280], P(('dp', 'seq'))
The draws below stay inside these ranges and needn't reach their ends.
Inputs may be any that keep to these rules, and one draw needn't show every extreme that they name: `lengths`: each clip's valid length; at least one clip has all 512 positions valid.
All inputs are finite; a program needn't handle non-finite values.
Results may differ from the reference program's by a relative error of at most 0.013.
Values may be sent and summed in bfloat16 or wider, within the bound.
No kernel may reach another device: no remote copies, remote signals or barrier semaphores. Data moves between devices by JAX's collectives and lax.ppermute only.
A program may use at most 384 MiB of HBM per device.

```python
import math
import jax
import jax.numpy as jnp
from jax import lax

D = 1280
HEADS = 16
HEAD = 80
FF = 5120
CLIP = 512
CLIPS = 16
TOKENS = 8192


def draw_lengths(key, part):
    key = jax.random.fold_in(key, 7)
    first_key, second_key = jax.random.split(key)
    drawn = jax.random.randint(first_key, (CLIPS,), CLIP // 2 + 1, CLIP + 1)
    longest = jax.random.randint(second_key, (), 0, CLIPS)
    return jnp.where(jnp.arange(CLIPS) == longest, CLIP, drawn).astype(jnp.int32)


def steps_of(key, shape, cuts, low, high):
    gain, own = 1.0, jax.random.fold_in(key, 6)
    for position, parts in cuts:
        heights = jnp.exp(jax.random.uniform(jax.random.fold_in(own, position), (parts,), jnp.float32, low / len(cuts), high / len(cuts)))
        gain = gain * jnp.repeat(heights, shape[position] // parts).reshape([-1 if axis == position else 1 for axis in range(len(shape))])
    return gain


def noise(key, extent, scale, bound, pieces=(), held_as=jnp.bfloat16):
    values = scale * jax.random.normal(key, extent, jnp.float32)
    if pieces:
        values = values * steps_of(key, extent, pieces, -0.22, 0.18)
    return jnp.clip(values, -bound, bound).astype(held_as)


def setup_inputs(seed: int = 0) -> dict:
    streams_of = jax.random.split(jax.random.key(seed), 19)
    return {
        "inputs": noise(streams_of[0], (TOKENS, D), 1.0, 6.0, ((0, 32),)),
        "lengths": draw_lengths(jax.random.fold_in(streams_of[18], 71), 0),
        "cotangent": noise(streams_of[2], (TOKENS, D), 1.0, 6.0, ((0, 32),)),
        "norm1_gain": jnp.clip(1.0 + 0.15 * jax.random.normal(streams_of[3], (D,), jnp.float32), 0.25, 1.75).astype(jnp.bfloat16),
        "norm1_shift": noise(streams_of[4], (D,), 0.3, 4.0, ((0, 16),)),
        "w_query": noise(streams_of[5], (D, D), D ** -0.5, 0.15625, ((0, 16),)),
        "b_query": noise(streams_of[6], (D,), 0.3, 4.0, ((0, 16),)),
        "w_key": noise(streams_of[7], (D, D), D ** -0.5, 0.15625, ((0, 16),)),
        "w_value": noise(streams_of[8], (D, D), D ** -0.5, 0.15625, ((0, 16),)),
        "b_value": noise(streams_of[9], (D,), 0.05, 0.75, ((0, 16),)),
        "w_output": noise(streams_of[10], (D, D), 4 ** -0.5, 3.0, ((0, 16),)),
        "b_output": noise(streams_of[11], (D,), 0.3, 4.0, ((0, 16),)),
        "norm2_gain": jnp.clip(1.0 + 0.15 * jax.random.normal(streams_of[12], (D,), jnp.float32), 0.25, 1.75).astype(jnp.bfloat16),
        "norm2_shift": noise(streams_of[13], (D,), 0.3, 4.0, ((0, 16),)),
        "w_up": noise(streams_of[14], (D, FF), D ** -0.5, 0.15625, ((0, 16),)),
        "b_up": noise(streams_of[15], (FF,), 0.3, 4.0, ((0, 16),)),
        "w_down": noise(streams_of[16], (FF, D), FF ** -0.5, 0.078125, ((0, 16),)),
        "b_down": noise(streams_of[17], (D,), 0.3, 4.0, ((0, 16),)),
    }


@jax.custom_vjp
def low(v):
    return lax.optimization_barrier(v.astype(jnp.bfloat16)).astype(jnp.float32)

@jax.custom_vjp
def low_back(v):
    return v

def low_keep(v):
    return (low(v), None)

def low_pass(kept, grad):
    return (grad,)

def back_keep(v):
    return (v, None)

def back_low(kept, grad):
    return (low(grad),)
low.defvjp(low_keep, low_pass)
low_back.defvjp(back_keep, back_low)
EPS_NORM = 1e-05
MASKED = -1e+30

def matmul(operand, weight):
    return jnp.dot(operand, weight, precision=lax.Precision.HIGHEST)

def layer_norm(values, norm_gain, norm_shift):
    average = lax.optimization_barrier(jnp.mean(values, axis=-1, keepdims=True))
    centred = values - average
    variance = lax.optimization_barrier(jnp.mean(centred * centred, axis=-1, keepdims=True))
    return centred * lax.rsqrt(variance + EPS_NORM) * norm_gain + norm_shift

def clip_forward(params, clip_inputs, length):
    norm1_gain, norm1_shift, w_query, b_query, w_key, w_value, b_value, w_output, b_output, norm2_gain, norm2_shift, w_up, b_up, w_down, b_down = params
    positions = jnp.arange(CLIP, dtype=jnp.int32)
    key_valid = positions < length
    normed1 = low(layer_norm(clip_inputs, norm1_gain, norm1_shift))
    queries = low(low_back(matmul(normed1, w_query) + b_query))
    keys = low(low_back(matmul(normed1, w_key)))
    values = low(low_back(matmul(normed1, w_value) + b_value))
    block_rows = min(512, CLIP)
    query_blocks = queries.reshape(CLIP // block_rows, block_rows, HEADS, HEAD)
    key_heads = keys.reshape(CLIP, HEADS, HEAD)
    value_heads = values.reshape(CLIP, HEADS, HEAD)
    score_scale = 1.0 / math.sqrt(HEAD)

    def attend(query_block):
        raw_scores = jnp.einsum('qhd,khd->hqk', query_block, key_heads, precision=lax.Precision.HIGHEST)
        scores = low_back(raw_scores * score_scale)
        scores = jnp.where(key_valid[None, None, :], scores, MASKED)
        probs = jax.nn.softmax(scores, axis=-1)
        return jnp.einsum('hqk,khd->qhd', low(probs), value_heads, precision=lax.Precision.HIGHEST)
    context = lax.map(jax.checkpoint(attend), query_blocks).reshape(CLIP, D)
    context = low(low_back(context))
    attended = low_back(matmul(context, w_output) + b_output)
    mid = clip_inputs + attended
    normed2 = low(layer_norm(mid, norm2_gain, norm2_shift))
    pre = low_back(matmul(normed2, w_up) + b_up)
    hidden = low(jax.nn.gelu(pre, approximate=False))
    branch = low_back(matmul(hidden, w_down) + b_down)
    return mid + branch

def reference(inputs, lengths, cotangent, norm1_gain, norm1_shift, w_query, b_query, w_key, w_value, b_value, w_output, b_output, norm2_gain, norm2_shift, w_up, b_up, w_down, b_down):
    params = (norm1_gain.astype(jnp.float32), norm1_shift.astype(jnp.float32), w_query.astype(jnp.float32), b_query.astype(jnp.float32), w_key.astype(jnp.float32), w_value.astype(jnp.float32), b_value.astype(jnp.float32), w_output.astype(jnp.float32), b_output.astype(jnp.float32), norm2_gain.astype(jnp.float32), norm2_shift.astype(jnp.float32), w_up.astype(jnp.float32), b_up.astype(jnp.float32), w_down.astype(jnp.float32), b_down.astype(jnp.float32))
    clip_inputs = inputs.astype(jnp.float32).reshape(CLIPS, CLIP, D)

    def forward(weights, clips_in):

        def one_clip(packed):
            return jax.checkpoint(clip_forward)(weights, packed[0], packed[1])
        return lax.map(one_clip, (clips_in, lengths))
    result, pullback = jax.vjp(forward, params, clip_inputs)
    positions = jnp.arange(CLIP, dtype=jnp.int32)
    row_valid = (positions[None, :] < lengths[:, None]).astype(jnp.float32)
    grad_out = cotangent.astype(jnp.float32).reshape(CLIPS, CLIP, D) * row_valid[:, :, None]
    grads, grad_inputs = pullback(grad_out)
    return (result.reshape(TOKENS, D).astype(jnp.bfloat16), grad_inputs.reshape(TOKENS, D), grads[0], grads[1], grads[2], grads[3], grads[4], grads[5], grads[6], grads[7], grads[8], grads[9], grads[10], grads[11], grads[12], grads[13], grads[14])
```

```python
import functools
import math

import jax
import jax.numpy as jnp
from jax import lax
from jax.experimental import pallas as pl
from jax.experimental.pallas import tpu as pltpu
from jax.sharding import PartitionSpec as P

HEAD = 80
EPS_NORM = 1e-05
MASKED = -1e30
RANKS = 4
AXES = ("dp", "seq")
BF16 = jnp.bfloat16
F32 = jnp.float32

CORE, ALONG_X, ALONG_Y, ALONG_Z, ALONG_Z2 = 1, 2, 4, 8, 16


def swap(values, mask, count):
    return lax.ppermute(values, AXES, [(place, place ^ mask) for place in range(count)])


def plane_route(planes):
    pairs = []
    for column in range(4):
        for plane in range(planes):
            for core in range(2):
                target_z = (plane >> 1) + 2 * core
                pairs.append(
                    (
                        (plane * 4 + column) * 2 + core,
                        (target_z * 4 + column) * 2 + (plane & 1),
                    )
                )
    return pairs


def move_blocks(arrays, moves, out_rows, place):
    columns = arrays[0].shape[1]

    def kernel(place_ref, *refs):
        in_refs, out_refs, sems = refs[: len(arrays)], refs[len(arrays) : -1], refs[-1]
        here = place_ref[0]
        copies = []
        for index, (array, source, out, target, rows) in enumerate(moves):
            source = pl.multiple_of(source(here), 8)
            target = pl.multiple_of(target(here), 8)
            copy = pltpu.make_async_copy(
                in_refs[array].at[pl.ds(source, rows)],
                out_refs[out].at[pl.ds(target, rows)],
                sems.at[index],
            )
            copy.start()
            copies.append(copy)
        for copy in copies:
            copy.wait()

    return pl.pallas_call(
        kernel,
        out_shape=[jax.ShapeDtypeStruct((rows, columns), arrays[0].dtype) for rows in out_rows],
        in_specs=[pl.BlockSpec(memory_space=pltpu.SMEM)]
        + [pl.BlockSpec(memory_space=pl.ANY)] * len(arrays),
        out_specs=[pl.BlockSpec(memory_space=pltpu.VMEM)] * len(out_rows),
        scratch_shapes=[pltpu.SemaphoreType.DMA((len(moves),))],
        compiler_params=pltpu.CompilerParams(vmem_limit_bytes=32 * 1024 * 1024),
    )(jnp.reshape(place, (1,)).astype(jnp.int32), *arrays)


def always(row):
    return lambda here: row


def xor_row(flip, rows, first=0, mask=15):
    return lambda here: jnp.bitwise_xor(jnp.bitwise_and(here, mask), flip) * rows + first


def tie(values, *others):
    return lax.optimization_barrier((values,) + others)[0]


def contract_rows(operand, other):
    return lax.dot_general(operand, other, (((0,), (0,)), ((), ())), preferred_element_type=F32)


def times_transposed(operand, weight):
    return lax.dot_general(operand, weight, (((1,), (1,)), ((), ())), preferred_element_type=F32)


def times(operand, weight):
    return jnp.dot(operand, weight, preferred_element_type=F32)


def column_sums(values):
    return jnp.sum(values.astype(F32), axis=0)


def normalize(values):
    average = jnp.mean(values, axis=-1, keepdims=True)
    centred = values - average
    inverse = lax.rsqrt(jnp.mean(centred * centred, axis=-1, keepdims=True) + EPS_NORM)
    return (centred * inverse, inverse)


def norm_backward(grad_normed, normalized, inverse, norm_gain):
    scaled = grad_normed * norm_gain
    return inverse * (
        scaled
        - jnp.mean(scaled, axis=-1, keepdims=True)
        - normalized * jnp.mean(scaled * normalized, axis=-1, keepdims=True)
    )


class Layout:
    def __init__(self, dp):
        self.dp = dp
        self.count = dp * 2
        self.planes = dp // 4
        self.direct = self.planes == 4
        self.dp_index = lax.axis_index("dp")
        self.core = lax.axis_index("seq")
        self.z = self.dp_index // 4
        self.y = (self.dp_index // 2) % 2
        self.x = self.dp_index % 2
        self.rank = (self.z % 2) * 2 + self.core

    def swap(self, values, mask):
        return swap(values, mask, self.count)

    def gather_tokens(self, values):
        other = self.swap(values, CORE)
        across = self.swap(values, ALONG_Z)
        across_other = self.swap(across, CORE)
        return jnp.concatenate([values, other, across, across_other], axis=0)

    def scatter_tokens(self, partial):
        rows = partial.shape[0] // 4
        blocks = partial.reshape(4, rows, partial.shape[1])
        far = self.swap(blocks[3].astype(BF16), CORE).astype(F32) + blocks[2]
        far = self.swap(far.astype(BF16), ALONG_Z)
        near = self.swap(blocks[1].astype(BF16), CORE)
        return blocks[0] + near.astype(F32) + far.astype(F32)

    def from_column(self, same, other):
        return (
            self.swap(other, ALONG_Z),
            self.swap(same, ALONG_Z2),
            self.swap(other, ALONG_Z | ALONG_Z2),
        )

    def spread_plane(self, first, second):
        first_x = self.swap(first, ALONG_X)
        second_y = self.swap(second, ALONG_Y)
        first_y = self.swap(jnp.concatenate([first, first_x]), ALONG_Y)
        second_x = self.swap(jnp.concatenate([second, second_y]), ALONG_X)
        return [first, first_x, first_y, second, second_y, second_x]

    def gather_columns(self, blocks):
        ranks, rows, columns = blocks.shape
        if not self.direct:
            whole = lax.all_gather(blocks, "dp", axis=0)
            mine = lax.dynamic_index_in_dim(whole, self.rank, 1, keepdims=False)
            return mine.reshape(self.dp * rows, columns)
        same = lax.dynamic_index_in_dim(blocks, self.rank, 0, keepdims=False)
        other = lax.dynamic_index_in_dim(blocks, self.rank ^ 2, 0, keepdims=False)
        by_1, by_2, by_3 = self.from_column(same, other)
        spread = self.spread_plane(jnp.concatenate([same, by_2]), jnp.concatenate([by_1, by_3]))
        return move_blocks(
            spread, self.column_moves(rows, 2 * rows, 0), [self.dp * rows], self.dp_index
        )[0]

    def column_moves(self, rows, stride, out):
        moves = []
        for far_z in range(2):
            first = far_z * rows
            for array, row, flip in (
                (0, first, 0),
                (1, first, 1),
                (2, first, 2),
                (2, stride + first, 3),
                (3, first, 4),
                (4, first, 6),
                (5, first, 5),
                (5, stride + first, 7),
            ):
                moves.append((array, always(row), out, xor_row(flip + 8 * far_z, rows), rows))
        return moves

    def gather_plane_rows(self, shard):
        rows, columns = shard.shape
        if not self.direct:
            whole = lax.all_gather(shard, "dp", axis=0, tiled=True)
            quarter = self.dp * rows // RANKS
            return lax.dynamic_slice_in_dim(whole, self.rank * quarter, quarter, 0)
        mine = lax.ppermute(shard, AXES, plane_route(self.planes))
        by_x = self.swap(mine, ALONG_X)
        by_y = self.swap(jnp.concatenate([mine, by_x]), ALONG_Y)
        sources = ((0, 0, 0), (1, 0, 1), (2, 0, 2), (2, rows, 3))
        moves = [
            (array, always(row), 0, xor_row(flip, rows, 0, 3), rows) for array, row, flip in sources
        ]
        return move_blocks([mine, by_x, by_y], moves, [4 * rows], self.dp_index)[0]

    def gather_feed_forward(self, w_up, w_down):
        shard, hidden = w_up.shape
        columns = hidden // RANKS
        rows, width = w_down.shape
        if not self.direct:
            blocks = w_up.reshape(shard, RANKS, columns).transpose(1, 0, 2)
            return self.gather_columns(blocks), self.gather_plane_rows(w_down)
        same = lax.dynamic_slice_in_dim(w_up, self.rank * columns, columns, 1)
        other = lax.dynamic_slice_in_dim(w_up, (self.rank ^ 2) * columns, columns, 1)
        by_1, by_2, by_3 = self.from_column(same, other)
        mine = lax.ppermute(w_down, AXES, plane_route(self.planes))
        half = rows // 2
        first = jnp.concatenate([same, by_2, mine[:half]])
        second = jnp.concatenate([by_1, by_3, mine[half:]])
        spread = self.spread_plane(first, second)
        stride = 2 * shard + half
        moves = self.column_moves(shard, stride, 0)
        for array, row, flip, upper in (
            (0, 0, 0, 0),
            (1, 0, 1, 0),
            (2, 0, 2, 0),
            (2, stride, 3, 0),
            (3, 0, 0, 1),
            (4, 0, 2, 1),
            (5, 0, 1, 1),
            (5, stride, 3, 1),
        ):
            source = always(row + 2 * shard)
            moves.append((array, source, 1, xor_row(flip, rows, upper * half, 3), half))
        return move_blocks(spread, moves, [self.dp * shard, 4 * rows], self.dp_index)

    def sum_plane(self, kept, sent, first_mask, second_mask):
        both = kept.astype(F32) + self.swap(sent, first_mask).astype(F32)
        rows = both.shape[0] // 2
        away = both[rows:].astype(BF16)
        return both[:rows] + self.swap(away, second_mask).astype(F32)

    def sum_column(self, blocks):
        steps, rows, columns = blocks.shape
        blocks = blocks.reshape(steps, 2, rows // 2, columns)
        mine = lax.dynamic_index_in_dim(blocks, self.core, 1, keepdims=False)
        away = lax.dynamic_index_in_dim(blocks, 1 - self.core, 1, keepdims=False).astype(BF16)
        both = jnp.stack([mine.astype(BF16), self.swap(away, CORE)], axis=1)
        by = [self.swap(both[step], step * ALONG_Z).astype(F32) for step in range(1, 4)]
        near = both[0].astype(F32) + by[1]
        far = by[0] + by[2]
        return self.in_rank_order([near[0], near[1], far[0], far[1]])

    def in_rank_order(self, ranks):
        high, low = self.rank // 2 == 1, self.rank % 2 == 1
        ranks = [jnp.where(low, ranks[i ^ 1], ranks[i]) for i in range(4)]
        return [jnp.where(high, ranks[i ^ 2], ranks[i]) for i in range(4)]

    def column_parts(self, rows, extra, array):
        moves = []
        half = 2 * rows + extra
        for out, flips in enumerate(((0, 1), (2, 3), (4, 6), (5, 7))):
            for block, flip in enumerate(flips):
                for far_z in range(2):
                    target = block * half + far_z * rows
                    moves.append(
                        (array, xor_row(flip + 8 * far_z, rows), out, always(target), rows)
                    )
        return moves

    def scatter_columns(self, grads):
        rows = grads.shape[0] // self.dp
        if not self.direct:
            return self.scatter_columns_plainly(grads)
        kept_1, sent_1, kept_2, sent_2 = move_blocks(
            [grads], self.column_parts(rows, 0, 0), [4 * rows] * 4, self.dp_index
        )
        first = self.sum_plane(kept_1, sent_1, ALONG_Y, ALONG_X)
        second = self.sum_plane(kept_2, sent_2, ALONG_X, ALONG_Y)
        return self.sum_column(
            jnp.stack([first[:rows], second[:rows], first[rows:], second[rows:]])
        )

    def scatter_columns_plainly(self, grads):
        dp, rows, columns = self.dp, grads.shape[0] // self.dp, grads.shape[1]
        whole = jnp.zeros((dp * rows, RANKS, columns), BF16)
        whole = lax.dynamic_update_slice_in_dim(whole, grads[:, None, :], self.rank, 1)
        mine = lax.psum_scatter(
            whole.reshape(dp * rows, RANKS * columns).astype(F32),
            AXES,
            scatter_dimension=0,
            tiled=True,
        )
        return [mine[:, rank * columns : (rank + 1) * columns] for rank in range(RANKS)]

    def scatter_plane_rows(self, grads):
        rows, columns = grads.shape
        if not self.direct:
            whole = jnp.zeros((RANKS, rows, columns), BF16)
            whole = lax.dynamic_update_slice_in_dim(whole, grads[None], self.rank, 0)
            return lax.psum_scatter(
                whole.reshape(RANKS * rows, columns).astype(F32),
                AXES,
                scatter_dimension=0,
                tiled=True,
            )
        rows //= 4
        moves = [
            (0, xor_row(flip, rows, 0, 3), flip // 2, always(flip % 2 * rows), rows)
            for flip in range(4)
        ]
        kept, sent = move_blocks([grads], moves, [2 * rows] * 2, self.dp_index)
        summed = self.sum_plane(kept, sent, ALONG_Y, ALONG_X)
        return self.sum_owners(summed[: rows // 2], summed[rows // 2 :])

    def sum_owners(self, lower, upper):
        back = [(target, source) for source, target in plane_route(self.planes)]
        crossed = [(source, target ^ CORE) for source, target in back]
        high = self.z // 2 == 1
        straight = jnp.where(high, upper, lower).astype(BF16)
        other = jnp.where(high, lower, upper).astype(BF16)
        return lax.ppermute(straight, AXES, back).astype(F32) + lax.ppermute(
            other, AXES, crossed
        ).astype(F32)

    def scatter_feed_forward(self, grad_up, grad_down):
        if not self.direct:
            return self.scatter_columns(grad_up), self.scatter_plane_rows(grad_down)
        shard = grad_up.shape[0] // self.dp
        rows = grad_down.shape[0] // 4
        half = rows // 2
        stride = 2 * shard + half
        moves = self.column_parts(shard, half, 0)
        for out, (flips, upper) in enumerate((((0, 1), 0), ((2, 3), 0), ((0, 2), 1), ((1, 3), 1))):
            for block, flip in enumerate(flips):
                target = always(block * stride + 2 * shard)
                moves.append((1, xor_row(flip, rows, upper * half, 3), out, target, half))
        kept_1, sent_1, kept_2, sent_2 = move_blocks(
            [grad_up, grad_down], moves, [2 * stride] * 4, self.dp_index
        )
        first = self.sum_plane(kept_1, sent_1, ALONG_Y, ALONG_X)
        second = self.sum_plane(kept_2, sent_2, ALONG_X, ALONG_Y)
        a, b = slice(0, shard), slice(shard, 2 * shard)
        columns = self.sum_column(jnp.stack([first[a], second[a], first[b], second[b]]))
        return columns, self.sum_owners(first[2 * shard :], second[2 * shard :])


def on_device(
    dp,
    inputs,
    lengths,
    cotangent,
    norm1_gain,
    norm1_shift,
    w_query,
    b_query,
    w_key,
    w_value,
    b_value,
    w_output,
    b_output,
    norm2_gain,
    norm2_shift,
    w_up,
    b_up,
    w_down,
    b_down,
):
    at = Layout(dp)
    tokens, width = inputs.shape
    shard = w_query.shape[0]
    hidden_width = w_up.shape[1]
    clip_rows = 2 * tokens
    rank_width = width // RANKS
    rank_heads = rank_width // HEAD
    rank_hidden = hidden_width // RANKS
    hidden_shard = hidden_width // dp

    positions = jnp.arange(tokens, dtype=jnp.int32)
    own_valid = (at.core * tokens + positions < lengths[0]).astype(F32)[:, None]
    grad_out = cotangent.astype(F32) * own_valid
    grad_branch = grad_out.astype(BF16)
    partner_length = at.swap(lengths, ALONG_Z)
    clip_positions = jnp.concatenate(
        [at.core * tokens + positions, (1 - at.core) * tokens + positions]
    )
    key_valid = jnp.stack([clip_positions < lengths[0], clip_positions < partner_length[0]])

    vectors = jnp.concatenate(
        [norm1_gain, norm1_shift, b_query, b_value, b_output, norm2_gain, norm2_shift, b_down, b_up]
    )
    extra = vectors.shape[0] // shard
    qkv = jnp.stack([w_query, w_key, w_value]).reshape(3, shard, RANKS, rank_width)
    qkv = qkv.transpose(2, 1, 0, 3).reshape(RANKS, shard, 3 * rank_width)
    vectors = jnp.broadcast_to(vectors.reshape(extra, shard).T[None], (RANKS, shard, extra))
    qkv = at.gather_columns(jnp.concatenate([qkv, vectors], axis=2))
    vectors = qkv[:, 3 * rank_width :].astype(F32)
    qkv = qkv[:, : 3 * rank_width]
    (gain1, shift1, bquery, bvalue, boutput, gain2, shift2, bdown) = (vectors[:, i] for i in range(8))
    bup = vectors[:, 8:].reshape(dp, shard, extra - 8).transpose(0, 2, 1).reshape(hidden_width)
    out_rows = at.gather_plane_rows(w_output)

    all_inputs = at.gather_tokens(inputs)
    normed1 = normalize(all_inputs.astype(F32))[0] * gain1 + shift1
    normed1 = normed1.astype(BF16)
    rank_slice = lambda vector, size: lax.dynamic_slice_in_dim(vector, at.rank * size, size)
    qkv_bias = jnp.concatenate(
        [
            rank_slice(bquery, rank_width),
            jnp.zeros((rank_width,), F32),
            rank_slice(bvalue, rank_width),
        ]
    )
    projected = (times(normed1, qkv) + qkv_bias).astype(BF16)
    heads = projected.reshape(2, clip_rows, 3, rank_heads, HEAD)
    query_heads, key_heads, value_heads = heads[:, :, 0], heads[:, :, 1], heads[:, :, 2]
    score_scale = 1.0 / math.sqrt(HEAD)
    scores = (
        jnp.einsum("bqhd,bkhd->bhqk", query_heads, key_heads, preferred_element_type=F32)
        * score_scale
    )
    scores = jnp.where(key_valid[:, None, None, :], scores, MASKED)
    highest = jnp.max(scores, axis=-1, keepdims=True)
    log_total = highest + jnp.log(jnp.sum(jnp.exp(scores - highest), axis=-1, keepdims=True))
    probabilities = jnp.exp(scores - log_total)
    low_probabilities = probabilities.astype(BF16)
    context = jnp.einsum(
        "bhqk,bkhd->bqhd", low_probabilities, value_heads, preferred_element_type=F32
    ).astype(BF16)
    context = context.reshape(2 * clip_rows, rank_width)
    attended = at.scatter_tokens(times(context, out_rows))

    up, down = at.gather_feed_forward(w_up, w_down)

    mid = inputs.astype(F32) + attended + boutput
    normalized2, inverse2 = normalize(mid)
    normed2 = at.gather_tokens((normalized2 * gain2 + shift2).astype(BF16))
    all_branch = at.gather_tokens(grad_branch)

    pre = times(normed2, up) + rank_slice(bup, rank_hidden)
    hidden, gelu_back = jax.vjp(lambda argument: jax.nn.gelu(argument, approximate=False), pre)
    hidden = hidden.astype(BF16)
    grad_pre = gelu_back(times_transposed(all_branch, down))[0].astype(BF16)
    grad_normed2 = at.scatter_tokens(times_transposed(grad_pre, up))
    grad_up = contract_rows(normed2, grad_pre).astype(BF16)
    grad_down = contract_rows(hidden, all_branch).astype(BF16)
    output = (mid + at.scatter_tokens(times(hidden, down)) + bdown).astype(BF16)

    grad_norm2_gain = jnp.sum(grad_normed2 * normalized2, axis=0)
    grad_norm2_shift = jnp.sum(grad_normed2, axis=0)
    grad_mid = grad_out + norm_backward(grad_normed2, normalized2, inverse2, gain2)
    grad_attended = grad_mid.astype(BF16)
    all_attended = at.gather_tokens(grad_attended)

    grad_context = times_transposed(all_attended, out_rows).astype(BF16)
    grad_context = grad_context.reshape(2, clip_rows, rank_heads, HEAD)
    grad_probs = jnp.einsum(
        "bqhd,bkhd->bhqk", grad_context, value_heads, preferred_element_type=F32
    )
    inner_sum = jnp.sum(probabilities * grad_probs, axis=-1, keepdims=True)
    grad_scores = (probabilities * (grad_probs - inner_sum)).astype(BF16)
    query_grad = (
        jnp.einsum("bhqk,bkhd->bqhd", grad_scores, key_heads, preferred_element_type=F32)
        * score_scale
    )
    key_grad = (
        jnp.einsum("bhqk,bqhd->bkhd", grad_scores, query_heads, preferred_element_type=F32)
        * score_scale
    )
    value_grad = jnp.einsum(
        "bhqk,bqhd->bkhd", low_probabilities, grad_context, preferred_element_type=F32
    )
    head_grads = [
        grad.reshape(2 * clip_rows, rank_width).astype(BF16)
        for grad in (query_grad, key_grad, value_grad)
    ]
    grad_projected = jnp.concatenate(head_grads, axis=1)
    grad_normed1 = at.scatter_tokens(times_transposed(grad_projected, qkv))
    grad_qkv = contract_rows(normed1, grad_projected).astype(BF16)
    grad_out_rows = contract_rows(context, all_attended).astype(BF16)

    normalized1, inverse1 = normalize(inputs.astype(F32))
    grad_norm1_gain = jnp.sum(grad_normed1 * normalized1, axis=0)
    grad_norm1_shift = jnp.sum(grad_normed1, axis=0)
    input_grad = grad_mid + norm_backward(grad_normed1, normalized1, inverse1, gain1)

    by_rank, grad_w_down = at.scatter_feed_forward(grad_up, grad_down)
    grad_w_up = jnp.concatenate(by_rank, axis=1)
    grad_w_output = at.scatter_plane_rows(grad_out_rows)

    def whole(part, size):
        return lax.dynamic_update_slice_in_dim(
            jnp.zeros((size,), F32), part, at.rank * (size // RANKS), 0
        )

    sums = [
        grad_norm1_gain,
        grad_norm1_shift,
        whole(column_sums(head_grads[0]), width),
        whole(column_sums(head_grads[2]), width),
        column_sums(grad_attended),
        grad_norm2_gain,
        grad_norm2_shift,
        column_sums(grad_branch),
    ]
    up_sums = whole(column_sums(grad_pre), hidden_width)
    half = shard // 2
    up_sums = up_sums.reshape(2 * dp, extra - 8, half).transpose(0, 2, 1).reshape(width, extra - 8)
    sums = jnp.concatenate([jnp.stack(sums, axis=1), up_sums], axis=1).astype(BF16)
    by_rank = at.scatter_columns(jnp.concatenate([grad_qkv, sums], axis=1))
    grad_w_query, grad_w_key, grad_w_value = (
        jnp.concatenate([part[:, i * rank_width : (i + 1) * rank_width] for part in by_rank], axis=1)
        for i in range(3)
    )
    sums = sum(part[:, 3 * rank_width :] for part in by_rank)
    shares = [sums[:, i] for i in range(8)] + [sums[:, 8:].T.reshape(-1)]
    return (
        output,
        input_grad,
        shares[0],
        shares[1],
        grad_w_query,
        shares[2],
        grad_w_key,
        grad_w_value,
        shares[3],
        grad_w_output,
        shares[4],
        shares[5],
        shares[6],
        grad_w_up,
        shares[8],
        grad_w_down,
        shares[7],
    )


def solution(mesh):
    rows, vector = P("dp", None), P("dp")
    own_rows, own_vector = P(AXES, None), P(AXES)
    return jax.shard_map(
        functools.partial(on_device, mesh.shape["dp"]),
        mesh=mesh,
        in_specs=(
            own_rows,
            vector,
            own_rows,
            vector,
            vector,
            rows,
            vector,
            rows,
            rows,
            vector,
            rows,
            vector,
            vector,
            vector,
            rows,
            vector,
            rows,
            vector,
        ),
        out_specs=(
            own_rows,
            own_rows,
            own_vector,
            own_vector,
            own_rows,
            own_vector,
            own_rows,
            own_rows,
            own_vector,
            own_rows,
            own_vector,
            own_vector,
            own_vector,
            own_rows,
            own_vector,
            own_rows,
            own_vector,
        ),
        check_vma=False,
    )
```

```python
import functools
import math

import jax
import jax.numpy as jnp
from jax import lax
from jax.experimental import pallas as pl
from jax.experimental.pallas import tpu as pltpu
from jax.sharding import PartitionSpec as P

HEAD = 80
EPS_NORM = 1e-05
MASKED = -1e30
RANKS = 4
AXES = ("dp", "seq")
BF16 = jnp.bfloat16
F32 = jnp.float32

CORE, ALONG_X, ALONG_Y, ALONG_Z, ALONG_Z2 = 1, 2, 4, 8, 16


def swap(values, mask, count):
    return lax.ppermute(values, AXES, [(place, place ^ mask) for place in range(count)])


def plane_route(planes):
    pairs = []
    for column in range(4):
        for plane in range(planes):
            for core in range(2):
                target_z = (plane >> 1) + 2 * core
                pairs.append(
                    (
                        (plane * 4 + column) * 2 + core,
                        (target_z * 4 + column) * 2 + (plane & 1),
                    )
                )
    return pairs


def move_blocks(arrays, moves, out_rows, place):
    columns = arrays[0].shape[1]

    def kernel(place_ref, *refs):
        in_refs, out_refs, sems = refs[: len(arrays)], refs[len(arrays) : -1], refs[-1]
        here = place_ref[0]
        copies = []
        for index, (array, source, out, target, rows) in enumerate(moves):
            source = pl.multiple_of(source(here), 8)
            target = pl.multiple_of(target(here), 8)
            copy = pltpu.make_async_copy(
                in_refs[array].at[pl.ds(source, rows)],
                out_refs[out].at[pl.ds(target, rows)],
                sems.at[index],
            )
            copy.start()
            copies.append(copy)
        for copy in copies:
            copy.wait()

    return pl.pallas_call(
        kernel,
        out_shape=[jax.ShapeDtypeStruct((rows, columns), arrays[0].dtype) for rows in out_rows],
        in_specs=[pl.BlockSpec(memory_space=pltpu.SMEM)]
        + [pl.BlockSpec(memory_space=pl.ANY)] * len(arrays),
        out_specs=[pl.BlockSpec(memory_space=pltpu.VMEM)] * len(out_rows),
        scratch_shapes=[pltpu.SemaphoreType.DMA((len(moves),))],
        compiler_params=pltpu.CompilerParams(vmem_limit_bytes=32 * 1024 * 1024),
    )(jnp.reshape(place, (1,)).astype(jnp.int32), *arrays)


def always(row):
    return lambda here: row


def xor_row(flip, rows, first=0, mask=15):
    return lambda here: jnp.bitwise_xor(jnp.bitwise_and(here, mask), flip) * rows + first


def tie(values, *others):
    return lax.optimization_barrier((values,) + others)[0]


def rows_times(operand, weight):
    return lax.dot_general(operand, weight, (((1,), (0,)), ((), ())), preferred_element_type=F32)


def times_transposed(operand, weight):
    return lax.dot_general(operand, weight, (((1,), (1,)), ((), ())), preferred_element_type=F32)


def contract_rows(operand, other):
    return lax.dot_general(operand, other, (((0,), (0,)), ((), ())), preferred_element_type=F32)


def normalize(values):
    average = jnp.mean(values, axis=-1, keepdims=True)
    centred = values - average
    inverse = lax.rsqrt(jnp.mean(centred * centred, axis=-1, keepdims=True) + EPS_NORM)
    return (centred * inverse, inverse)


def norm_backward(grad_normed, normalized, inverse, norm_gain):
    scaled = grad_normed * norm_gain
    return inverse * (
        scaled
        - jnp.mean(scaled, axis=-1, keepdims=True)
        - normalized * jnp.mean(scaled * normalized, axis=-1, keepdims=True)
    )


def column_sums(values):
    return jnp.sum(values.astype(F32), axis=0, keepdims=True)


def local_call(kernel, outs, *operands, flops=0, scratch=(), limit=32):
    vmem = pl.BlockSpec(memory_space=pltpu.VMEM)
    shapes = [jax.ShapeDtypeStruct(shape, dtype) for shape, dtype in outs]
    moved = sum(math.prod(shape) * jnp.dtype(dtype).itemsize for shape, dtype in outs)
    moved += sum(operand.size * operand.dtype.itemsize for operand in operands)
    return pl.pallas_call(
        kernel,
        out_shape=shapes,
        in_specs=[pl.BlockSpec(memory_space=pltpu.SMEM)] + [vmem] * (len(operands) - 1),
        out_specs=[vmem] * len(outs),
        scratch_shapes=list(scratch),
        compiler_params=pltpu.CompilerParams(vmem_limit_bytes=limit * 1024 * 1024),
        cost_estimate=pl.CostEstimate(flops=flops * 20, bytes_accessed=moved * 20, transcendentals=0),
    )(*operands)


CHUNK = 64


def row_chunks(rows):
    return [slice(first, min(first + CHUNK, rows)) for first in range(0, rows, CHUNK)]


def head_slice(part, head, heads):
    first = (part * heads + head) * HEAD
    return slice(first, first + HEAD)


def cut_projections(place, w_query, w_key, w_value, vectors):
    shard, width = w_query.shape
    rank_width = width // RANKS
    extra = vectors.shape[0]
    columns = 3 * rank_width + extra

    def kernel(place_ref, query_ref, key_ref, value_ref, vectors_ref, same_ref, other_ref, blocks):
        turned = vectors_ref[...].T.astype(BF16)
        for rank in range(RANKS):
            cut = slice(rank * rank_width, (rank + 1) * rank_width)
            for part, ref in enumerate((query_ref, key_ref, value_ref)):
                blocks[rank, :, part * rank_width : (part + 1) * rank_width] = ref[:, cut]
            blocks[rank, :, 3 * rank_width :] = turned
        same_ref[...] = blocks[place_ref[1]]
        other_ref[...] = blocks[jnp.bitwise_xor(place_ref[1], 2)]

    return local_call(
        kernel,
        [((shard, columns), BF16)] * 2,
        place,
        w_query,
        w_key,
        w_value,
        vectors,
        scratch=[pltpu.VMEM((RANKS, shard, columns), BF16)],
    )


def attention_forward(place, clip, inputs, qkv, vectors, out_rows):
    half, width = inputs[0].shape
    rows = 2 * half
    rank_width = width // RANKS
    heads = rank_width // HEAD
    scale = 1.0 / math.sqrt(HEAD)

    def kernel(
        place_ref,
        first_ref,
        second_ref,
        qkv_ref,
        vectors_ref,
        out_rows_ref,
        normed_ref,
        projected_ref,
        context_ref,
        kept_ref,
        sent_ref,
    ):
        core, rank, length = place_ref[0], place_ref[1], place_ref[2 + clip]
        gain, shift = vectors_ref[0:1, :], vectors_ref[1:2, :]
        for index, ref in enumerate((first_ref, second_ref)):
            for cut in row_chunks(half):
                normed = normalize(ref[cut, :].astype(F32))[0] * gain + shift
                normed_ref[index * half + cut.start : index * half + cut.stop, :] = normed.astype(
                    BF16
                )
        bias = jnp.zeros((1, rank_width), F32)
        value_bias = bias
        for other in range(RANKS):
            cut = slice(other * rank_width, (other + 1) * rank_width)
            bias += jnp.where(rank == other, vectors_ref[2:3, cut], 0.0)
            value_bias += jnp.where(rank == other, vectors_ref[3:4, cut], 0.0)
        biases = (bias, None, value_bias)
        projected = rows_times(normed_ref[...], qkv_ref[...])
        for part, added in enumerate(biases):
            values = projected[:, part * rank_width : (part + 1) * rank_width]
            values = values if added is None else values + added
            projected_ref[:, part * rank_width : (part + 1) * rank_width] = values.astype(BF16)
        positions = lax.broadcasted_iota(jnp.int32, (rows, rows), 1)
        positions = jnp.bitwise_and(positions + core * half, rows - 1)
        valid = positions < length
        for head in range(heads):
            queries = projected_ref[:, head_slice(0, head, heads)]
            keys = projected_ref[:, head_slice(1, head, heads)]
            values = projected_ref[:, head_slice(2, head, heads)]
            scores = jnp.where(valid, times_transposed(queries, keys) * scale, MASKED)
            weights = jnp.exp(scores - jnp.max(scores, axis=1, keepdims=True))
            weights = weights * (1.0 / jnp.sum(weights, axis=1, keepdims=True))
            context = rows_times(weights.astype(BF16), values)
            context_ref[:, head_slice(0, head, heads)] = context.astype(BF16)
        kept_ref[...] = rows_times(context_ref[0:half, :], out_rows_ref[...])
        sent_ref[...] = rows_times(context_ref[half:rows, :], out_rows_ref[...]).astype(BF16)

    return local_call(
        kernel,
        [
            ((rows, width), BF16),
            ((rows, 3 * rank_width), BF16),
            ((rows, rank_width), BF16),
            ((half, width), F32),
            ((half, width), BF16),
        ],
        place,
        *inputs,
        qkv,
        vectors,
        out_rows,
        flops=2 * rows * width * width + 4 * rows * rows * rank_width,
    )


def attention_backward(place, clip, grads, inputs, projected, qkv, vectors, out_rows):
    half, width = inputs[0].shape
    rows = 2 * half
    rank_width = width // RANKS
    heads = rank_width // HEAD
    scale = 1.0 / math.sqrt(HEAD)

    def kernel(
        place_ref,
        grad_first_ref,
        grad_second_ref,
        first_ref,
        second_ref,
        projected_ref,
        qkv_ref,
        vectors_ref,
        out_rows_ref,
        grads_ref,
        kept_ref,
        sent_ref,
        norm_sums_ref,
        head_sums_ref,
        context_ref,
        normed_ref,
    ):
        core, length = place_ref[0], place_ref[2 + clip]
        for index, ref in enumerate((grad_first_ref, grad_second_ref)):
            context_ref[index * half : (index + 1) * half, :] = times_transposed(
                ref[...], out_rows_ref[...]
            ).astype(BF16)
        positions = lax.broadcasted_iota(jnp.int32, (rows, rows), 0)
        positions = jnp.bitwise_and(positions + core * half, rows - 1)
        valid = positions < length
        for head in range(heads):
            queries = projected_ref[:, head_slice(0, head, heads)]
            keys = projected_ref[:, head_slice(1, head, heads)]
            values = projected_ref[:, head_slice(2, head, heads)]
            grad_context = context_ref[:, head_slice(0, head, heads)]
            scores = jnp.where(valid, times_transposed(keys, queries) * scale, MASKED)
            weights = jnp.exp(scores - jnp.max(scores, axis=0, keepdims=True))
            weights = weights * (1.0 / jnp.sum(weights, axis=0, keepdims=True))
            grad_weights = times_transposed(values, grad_context)
            inner = jnp.sum(weights * grad_weights, axis=0, keepdims=True)
            grad_scores = (weights * (grad_weights - inner)).astype(BF16)
            grad_query = contract_rows(grad_scores, keys) * scale
            grad_key = rows_times(grad_scores, queries) * scale
            grad_value = rows_times(weights.astype(BF16), grad_context)
            grads_ref[:, head_slice(0, head, heads)] = grad_query.astype(BF16)
            grads_ref[:, head_slice(1, head, heads)] = grad_key.astype(BF16)
            grads_ref[:, head_slice(2, head, heads)] = grad_value.astype(BF16)
        head_sums_ref[...] = column_sums(grads_ref[...])
        weight = qkv_ref[:, 0 : 3 * rank_width]
        gain_sum = jnp.zeros((1, width), F32)
        shift_sum = jnp.zeros((1, width), F32)
        for index, ref in enumerate((first_ref, second_ref)):
            normed_ref[...] = times_transposed(
                grads_ref[index * half : (index + 1) * half, :], weight
            )
            for cut in row_chunks(half):
                grad = normed_ref[cut, :]
                if index == 0:
                    kept_ref[cut, :] = grad
                else:
                    sent_ref[cut, :] = grad.astype(BF16)
                gain_sum += column_sums(grad * normalize(ref[cut, :].astype(F32))[0])
                shift_sum += column_sums(grad)
        norm_sums_ref[0:1, :] = gain_sum
        norm_sums_ref[1:2, :] = shift_sum

    return local_call(
        kernel,
        [
            ((rows, 3 * rank_width), BF16),
            ((half, width), F32),
            ((half, width), BF16),
            ((2, width), F32),
            ((1, 3 * rank_width), F32),
        ],
        place,
        *grads,
        *inputs,
        projected,
        qkv,
        vectors,
        out_rows,
        flops=2 * rows * width * width + 10 * rows * rows * rank_width,
        scratch=[pltpu.VMEM((rows, rank_width), BF16), pltpu.VMEM((half, width), F32)],
    )


def feed_forward(place, normed, branch, up, down, up_bias):
    half, width = normed[0].shape
    rows = 2 * half
    hidden_width = up.shape[1]
    chunk = 256

    def kernel(
        place_ref,
        first_ref,
        second_ref,
        branch_first_ref,
        branch_second_ref,
        up_ref,
        down_ref,
        bias_ref,
        hidden_ref,
        grad_ref,
        sums_ref,
        kept_ref,
        sent_ref,
    ):
        for begin in range(0, hidden_width, chunk):
            cut = slice(begin, begin + chunk)
            total = jnp.zeros((1, chunk), F32)
            for index, (ref, branch_ref) in enumerate(
                ((first_ref, branch_first_ref), (second_ref, branch_second_ref))
            ):
                here = slice(index * half, (index + 1) * half)
                pre = rows_times(ref[...], up_ref[:, cut]) + bias_ref[:, cut]
                grad_hidden = times_transposed(branch_ref[...], down_ref[cut, :])
                share = 0.5 * (1.0 + lax.erf(pre * math.sqrt(0.5)))
                hidden_ref[here, cut] = (pre * share).astype(BF16)
                slope = share + pre * (jnp.exp(-0.5 * pre * pre) * (1.0 / math.sqrt(2.0 * math.pi)))
                grad = (grad_hidden * slope).astype(BF16)
                grad_ref[here, cut] = grad
                total += column_sums(grad)
            sums_ref[:, cut] = total
        kept_ref[...] = times_transposed(grad_ref[0:half, :], up_ref[...])
        sent_ref[...] = times_transposed(grad_ref[half:rows, :], up_ref[...]).astype(BF16)

    return local_call(
        kernel,
        [
            ((rows, hidden_width), BF16),
            ((rows, hidden_width), BF16),
            ((1, hidden_width), F32),
            ((half, width), F32),
            ((half, width), BF16),
        ],
        place,
        *normed,
        *branch,
        up,
        down,
        up_bias,
        flops=6 * rows * width * hidden_width,
    )


def feed_forward_out(place, hidden, down):
    rows, width = hidden.shape[0], down.shape[1]
    half = rows // 2

    def kernel(place_ref, hidden_ref, down_ref, kept_ref, sent_ref):
        kept_ref[...] = rows_times(hidden_ref[0:half, :], down_ref[...])
        sent_ref[...] = rows_times(hidden_ref[half:rows, :], down_ref[...]).astype(BF16)

    return local_call(
        kernel,
        [((half, width), F32), ((half, width), BF16)],
        place,
        hidden,
        down,
        flops=2 * rows * hidden.shape[1] * width,
    )


def sort_rows(here, source_ref, out_refs, moves, array):
    for which, source, out, target, rows in moves:
        if which == array:
            first = pl.multiple_of(source(here), 16)
            out_refs[out][target(here) : target(here) + rows, :] = source_ref[pl.ds(first, rows), :]


def feed_forward_grads(place, hidden, grad_pre, normed, branch, moves, out_rows):
    half, width = normed[0].shape
    hidden_width = hidden[0].shape[1]

    def kernel(place_ref, *refs):
        hidden_refs, grad_refs = refs[0:2], refs[2:4]
        normed_refs, branch_refs = refs[4:8], refs[8:12]
        out_refs = refs[12:-2] if moves else refs[12:]
        up_ref, down_ref = refs[-2:] if moves else out_refs
        for target, lefts, rights in (
            (up_ref, normed_refs, grad_refs),
            (down_ref, hidden_refs, branch_refs),
        ):
            for begin in range(0, target.shape[0], 256):
                cut = slice(begin, begin + 256)
                total = 0.0
                for quarter in range(4):
                    rows = slice((quarter % 2) * half, (quarter % 2 + 1) * half)
                    if target is up_ref:
                        left, right = lefts[quarter][:, cut], rights[quarter // 2][rows, :]
                    else:
                        left, right = lefts[quarter // 2][rows, cut], rights[quarter][...]
                    total = total + contract_rows(left, right)
                target[cut, :] = total.astype(BF16)
        if moves:
            sort_rows(place_ref[4], up_ref, out_refs, moves, 0)
            sort_rows(place_ref[4], down_ref, out_refs, moves, 1)

    whole = [((width, hidden_width), BF16), ((hidden_width, width), BF16)]
    return local_call(
        kernel,
        [((rows, width), BF16) for rows in out_rows] if moves else whole,
        place,
        *hidden,
        *grad_pre,
        *normed,
        *branch,
        flops=16 * half * width * hidden_width,
        scratch=[pltpu.VMEM(shape, dtype) for shape, dtype in whole] if moves else [],
    )


def attention_grads(place, normed, grads, context, attended, sums, rank_sums, moves, out_rows):
    rows, width = normed[0].shape
    half = rows // 2
    rank_width = width // RANKS
    extra = sums.shape[0]
    columns = 3 * rank_width + extra
    column_moves, plane_moves = moves
    count = len(out_rows[0]) if column_moves else 1

    def kernel(place_ref, *refs):
        normed_refs, grad_refs, context_refs = refs[0:2], refs[2:4], refs[4:6]
        attended_refs, sums_ref, rank_ref = refs[6:10], refs[10], refs[11]
        outs = refs[12:-3] if column_moves else refs[12:-1]
        total_ref = refs[-1]
        rank = place_ref[1]
        target = refs[-3] if column_moves else outs[0]
        for begin in range(0, width, 256):
            cut = slice(begin, begin + 256)
            total = contract_rows(normed_refs[0][:, cut], grad_refs[0][...])
            total += contract_rows(normed_refs[1][:, cut], grad_refs[1][...])
            target[cut, 0 : 3 * rank_width] = total.astype(BF16)
        for other in range(RANKS):
            cut = slice(other * rank_width, (other + 1) * rank_width)
            total_ref[:, cut] = sums_ref[:, cut] + jnp.where(rank == other, rank_ref[...], 0.0)
        target[:, 3 * rank_width :] = total_ref[...].T.astype(BF16)
        total = 0.0
        for quarter in range(4):
            cut = slice((quarter % 2) * half, (quarter % 2 + 1) * half)
            total = total + contract_rows(
                context_refs[quarter // 2][cut, :], attended_refs[quarter][...]
            )
        plane_target = refs[-2] if column_moves else outs[1]
        plane_target[...] = total.astype(BF16)
        if column_moves:
            sort_rows(place_ref[4], target, outs[:count], column_moves, 0)
            sort_rows(place_ref[4], plane_target, outs[count:], plane_moves, 0)

    whole = [((width, columns), BF16), ((rank_width, width), BF16)]
    if column_moves:
        outs = [((rows_, columns), BF16) for rows_ in out_rows[0]]
        outs += [((rows_, width), BF16) for rows_ in out_rows[1]]
    else:
        outs = whole
    scratch = [pltpu.VMEM(shape, dtype) for shape, dtype in whole] if column_moves else []
    return local_call(
        kernel,
        outs,
        place,
        *normed,
        *grads,
        *context,
        *attended,
        sums,
        rank_sums,
        flops=4 * rows * width * columns + 4 * rows * rank_width * width,
        scratch=scratch + [pltpu.VMEM((extra, width), F32)],
    )


def norm_forward(place, inputs, shares, vectors):
    rows, width = inputs.shape

    def kernel(place_ref, inputs_ref, kept_ref, near_ref, far_ref, vectors_ref, mid_ref, normed_ref):
        for cut in row_chunks(rows):
            attended = kept_ref[cut, :] + near_ref[cut, :].astype(F32)
            attended += far_ref[cut, :].astype(F32)
            mid = inputs_ref[cut, :].astype(F32) + attended + vectors_ref[4:5, :]
            mid_ref[cut, :] = mid
            normed = normalize(mid)[0] * vectors_ref[5:6, :] + vectors_ref[6:7, :]
            normed_ref[cut, :] = normed.astype(BF16)

    return local_call(
        kernel, [((rows, width), F32), ((rows, width), BF16)], place, inputs, *shares, vectors
    )


def norm_grads(place, residual, values, shares, vectors, gain_row, with_sums):
    rows, width = residual.shape

    def kernel(
        place_ref, residual_ref, values_ref, kept_ref, near_ref, far_ref, vectors_ref, *out_refs
    ):
        totals = [jnp.zeros((1, width), F32)] * 3
        for cut in row_chunks(rows):
            grad = kept_ref[cut, :] + near_ref[cut, :].astype(F32)
            grad += far_ref[cut, :].astype(F32)
            normalized, inverse = normalize(values_ref[cut, :].astype(F32))
            gain = vectors_ref[gain_row : gain_row + 1, :]
            result = residual_ref[cut, :] + norm_backward(grad, normalized, inverse, gain)
            out_refs[0][cut, :] = result
            if with_sums:
                rounded = result.astype(BF16)
                out_refs[1][cut, :] = rounded
                terms = (grad * normalized, grad, rounded)
                totals = [total + column_sums(term) for total, term in zip(totals, terms)]
        if with_sums:
            for row, total in enumerate(totals):
                out_refs[2][row : row + 1, :] = total

    outs = [((rows, width), F32)]
    if with_sums:
        outs += [((rows, width), BF16), ((3, width), F32)]
    return local_call(kernel, outs, place, residual, values, *shares, vectors)


class Layout:
    def __init__(self, dp):
        self.dp = dp
        self.count = dp * 2
        self.planes = dp // 4
        self.direct = self.planes == 4
        self.dp_index = lax.axis_index("dp")
        self.core = lax.axis_index("seq")
        self.z = self.dp_index // 4
        self.y = (self.dp_index // 2) % 2
        self.x = self.dp_index % 2
        self.rank = (self.z % 2) * 2 + self.core

    def swap(self, values, mask):
        return swap(values, mask, self.count)

    def gather_tokens(self, values):
        across = self.swap(values, ALONG_Z)
        return (values, self.swap(values, CORE)), (across, self.swap(across, CORE))

    def scatter_tokens(self, own, far):
        crossing = (far[0] + self.swap(far[1], CORE).astype(F32)).astype(BF16)
        return own[0], self.swap(own[1], CORE), self.swap(crossing, ALONG_Z)

    def from_column(self, same, other):
        return (
            self.swap(other, ALONG_Z),
            self.swap(same, ALONG_Z2),
            self.swap(other, ALONG_Z | ALONG_Z2),
        )

    def spread_plane(self, first, second):
        first_x = self.swap(first, ALONG_X)
        second_y = self.swap(second, ALONG_Y)
        first_y = self.swap(jnp.concatenate([first, first_x]), ALONG_Y)
        second_x = self.swap(jnp.concatenate([second, second_y]), ALONG_X)
        return [first, first_x, first_y, second, second_y, second_x]

    def gather_columns(self, same, other):
        rows, columns = same.shape
        if not self.direct:
            return self.gather_columns_plainly(same, other)
        by_1, by_2, by_3 = self.from_column(same, other)
        spread = self.spread_plane(jnp.concatenate([same, by_2]), jnp.concatenate([by_1, by_3]))
        return move_blocks(
            spread, self.column_moves(rows, 2 * rows, 0), [self.dp * rows], self.dp_index
        )[0]

    def gather_columns_plainly(self, same, other):
        low = self.rank < 2
        both = jnp.stack([jnp.where(low, same, other), jnp.where(low, other, same)])
        whole = lax.all_gather(both, "dp", axis=0)
        mine = lax.dynamic_index_in_dim(whole, self.rank // 2, 1, keepdims=False)
        return mine.reshape(-1, same.shape[1])

    def column_moves(self, rows, stride, out):
        moves = []
        for far_z in range(2):
            first = far_z * rows
            for array, row, flip in (
                (0, first, 0),
                (1, first, 1),
                (2, first, 2),
                (2, stride + first, 3),
                (3, first, 4),
                (4, first, 6),
                (5, first, 5),
                (5, stride + first, 7),
            ):
                moves.append((array, always(row), out, xor_row(flip + 8 * far_z, rows), rows))
        return moves

    def gather_plane_rows(self, shard):
        rows, columns = shard.shape
        if not self.direct:
            whole = lax.all_gather(shard, "dp", axis=0, tiled=True)
            quarter = self.dp * rows // RANKS
            return lax.dynamic_slice_in_dim(whole, self.rank * quarter, quarter, 0)
        mine = lax.ppermute(shard, AXES, plane_route(self.planes))
        by_x = self.swap(mine, ALONG_X)
        by_y = self.swap(jnp.concatenate([mine, by_x]), ALONG_Y)
        sources = ((0, 0, 0), (1, 0, 1), (2, 0, 2), (2, rows, 3))
        moves = [
            (array, always(row), 0, xor_row(flip, rows, 0, 3), rows) for array, row, flip in sources
        ]
        return move_blocks([mine, by_x, by_y], moves, [4 * rows], self.dp_index)[0]

    def gather_feed_forward(self, w_up, w_down):
        shard, hidden = w_up.shape
        columns = hidden // RANKS
        rows, width = w_down.shape
        same = lax.dynamic_slice_in_dim(w_up, self.rank * columns, columns, 1)
        other = lax.dynamic_slice_in_dim(w_up, (self.rank ^ 2) * columns, columns, 1)
        if not self.direct:
            return self.gather_columns_plainly(same, other), self.gather_plane_rows(w_down)
        by_1, by_2, by_3 = self.from_column(same, other)
        mine = lax.ppermute(w_down, AXES, plane_route(self.planes))
        half = rows // 2
        first = jnp.concatenate([same, by_2, mine[:half]])
        second = jnp.concatenate([by_1, by_3, mine[half:]])
        spread = self.spread_plane(first, second)
        stride = 2 * shard + half
        moves = self.column_moves(shard, stride, 0)
        for array, row, flip, upper in (
            (0, 0, 0, 0),
            (1, 0, 1, 0),
            (2, 0, 2, 0),
            (2, stride, 3, 0),
            (3, 0, 0, 1),
            (4, 0, 2, 1),
            (5, 0, 1, 1),
            (5, stride, 3, 1),
        ):
            source = always(row + 2 * shard)
            moves.append((array, source, 1, xor_row(flip, rows, upper * half, 3), half))
        return move_blocks(spread, moves, [self.dp * shard, 4 * rows], self.dp_index)

    def sum_plane(self, kept, sent, first_mask, second_mask):
        both = kept.astype(F32) + self.swap(sent, first_mask).astype(F32)
        rows = both.shape[0] // 2
        away = both[rows:].astype(BF16)
        return both[:rows] + self.swap(away, second_mask).astype(F32)

    def sum_column(self, blocks):
        steps, rows, columns = blocks.shape
        blocks = blocks.reshape(steps, 2, rows // 2, columns)
        mine = lax.dynamic_index_in_dim(blocks, self.core, 1, keepdims=False)
        away = lax.dynamic_index_in_dim(blocks, 1 - self.core, 1, keepdims=False).astype(BF16)
        both = jnp.stack([mine.astype(BF16), self.swap(away, CORE)], axis=1)
        by = [self.swap(both[step], step * ALONG_Z).astype(F32) for step in range(1, 4)]
        near = both[0].astype(F32) + by[1]
        far = by[0] + by[2]
        return self.in_rank_order([near[0], near[1], far[0], far[1]])

    def in_rank_order(self, ranks):
        high, low = self.rank // 2 == 1, self.rank % 2 == 1
        ranks = [jnp.where(low, ranks[i ^ 1], ranks[i]) for i in range(4)]
        return [jnp.where(high, ranks[i ^ 2], ranks[i]) for i in range(4)]

    def column_parts(self, rows, extra, array):
        moves = []
        half = 2 * rows + extra
        for out, flips in enumerate(((0, 1), (2, 3), (4, 6), (5, 7))):
            for block, flip in enumerate(flips):
                for far_z in range(2):
                    target = block * half + far_z * rows
                    moves.append(
                        (array, xor_row(flip + 8 * far_z, rows), out, always(target), rows)
                    )
        return moves

    def column_order(self, rows):
        return (self.column_parts(rows, 0, 0), [4 * rows] * 4) if self.direct else ([], [])

    def scatter_columns(self, sorted_grads):
        if not self.direct:
            return self.scatter_columns_plainly(sorted_grads[0])
        kept_1, sent_1, kept_2, sent_2 = sorted_grads
        rows = kept_1.shape[0] // 4
        first = self.sum_plane(kept_1, sent_1, ALONG_Y, ALONG_X)
        second = self.sum_plane(kept_2, sent_2, ALONG_X, ALONG_Y)
        return self.sum_column(
            jnp.stack([first[:rows], second[:rows], first[rows:], second[rows:]])
        )

    def scatter_columns_plainly(self, grads):
        dp, rows, columns = self.dp, grads.shape[0] // self.dp, grads.shape[1]
        whole = jnp.zeros((dp * rows, RANKS, columns), BF16)
        whole = lax.dynamic_update_slice_in_dim(whole, grads[:, None, :], self.rank, 1)
        mine = lax.psum_scatter(
            whole.reshape(dp * rows, RANKS * columns).astype(F32),
            AXES,
            scatter_dimension=0,
            tiled=True,
        )
        return [mine[:, rank * columns : (rank + 1) * columns] for rank in range(RANKS)]

    def plane_order(self, rows):
        if not self.direct:
            return [], []
        moves = [
            (0, xor_row(flip, rows, 0, 3), flip // 2, always(flip % 2 * rows), rows)
            for flip in range(4)
        ]
        return moves, [2 * rows] * 2

    def scatter_plane_rows(self, sorted_grads):
        if not self.direct:
            (grads,) = sorted_grads
            rows, columns = grads.shape
            whole = jnp.zeros((RANKS, rows, columns), BF16)
            whole = lax.dynamic_update_slice_in_dim(whole, grads[None], self.rank, 0)
            return lax.psum_scatter(
                whole.reshape(RANKS * rows, columns).astype(F32),
                AXES,
                scatter_dimension=0,
                tiled=True,
            )
        summed = self.sum_plane(*sorted_grads, ALONG_Y, ALONG_X)
        rows = summed.shape[0]
        return self.sum_owners(summed[: rows // 2], summed[rows // 2 :])

    def sum_owners(self, lower, upper):
        back = [(target, source) for source, target in plane_route(self.planes)]
        crossed = [(source, target ^ CORE) for source, target in back]
        high = self.z // 2 == 1
        straight = jnp.where(high, upper, lower).astype(BF16)
        other = jnp.where(high, lower, upper).astype(BF16)
        return lax.ppermute(straight, AXES, back).astype(F32) + lax.ppermute(
            other, AXES, crossed
        ).astype(F32)

    def feed_forward_order(self, shard, rows):
        if not self.direct:
            return [], []
        half = rows // 2
        stride = 2 * shard + half
        moves = self.column_parts(shard, half, 0)
        for out, (flips, upper) in enumerate((((0, 1), 0), ((2, 3), 0), ((0, 2), 1), ((1, 3), 1))):
            for block, flip in enumerate(flips):
                target = always(block * stride + 2 * shard)
                moves.append((1, xor_row(flip, rows, upper * half, 3), out, target, half))
        return moves, [2 * stride] * 4

    def scatter_feed_forward(self, sorted_grads, shard):
        if not self.direct:
            grad_up, grad_down = sorted_grads
            return self.scatter_columns([grad_up]), self.scatter_plane_rows([grad_down])
        kept_1, sent_1, kept_2, sent_2 = sorted_grads
        first = self.sum_plane(kept_1, sent_1, ALONG_Y, ALONG_X)
        second = self.sum_plane(kept_2, sent_2, ALONG_X, ALONG_Y)
        a, b = slice(0, shard), slice(shard, 2 * shard)
        columns = self.sum_column(jnp.stack([first[a], second[a], first[b], second[b]]))
        return columns, self.sum_owners(first[2 * shard :], second[2 * shard :])


def on_device(
    dp,
    inputs,
    lengths,
    cotangent,
    norm1_gain,
    norm1_shift,
    w_query,
    b_query,
    w_key,
    w_value,
    b_value,
    w_output,
    b_output,
    norm2_gain,
    norm2_shift,
    w_up,
    b_up,
    w_down,
    b_down,
):
    at = Layout(dp)
    tokens, width = inputs.shape
    shard = w_query.shape[0]
    hidden_width = w_up.shape[1]
    rank_width = width // RANKS
    rank_hidden = hidden_width // RANKS

    partner_length = at.swap(lengths, ALONG_Z)
    place = jnp.stack([at.core, at.rank, lengths[0], partner_length[0], at.dp_index])
    place = place.astype(jnp.int32)
    here = jnp.stack([at.core, at.rank]).astype(jnp.int32)

    vectors = jnp.concatenate(
        [norm1_gain, norm1_shift, b_query, b_value, b_output, norm2_gain, norm2_shift, b_down, b_up]
    )
    extra = vectors.shape[0] // shard
    vectors = vectors.reshape(extra, shard).astype(F32)
    same, other = cut_projections(here, w_query, w_key, w_value, vectors)
    own_inputs, far_inputs = at.gather_tokens(inputs)
    qkv = at.gather_columns(same, other)
    vectors = qkv[:, 3 * rank_width :].astype(F32).T
    up_bias = vectors[8:].reshape(extra - 8, dp, shard).transpose(1, 0, 2).reshape(1, hidden_width)
    up_bias = lax.dynamic_slice_in_dim(up_bias, at.rank * rank_hidden, rank_hidden, 1)
    out_rows = at.gather_plane_rows(w_output)

    far_clip = attention_forward(place, 1, far_inputs, qkv, vectors, out_rows)
    own_clip = attention_forward(place, 0, own_inputs, qkv, vectors, out_rows)
    shares = at.scatter_tokens(own_clip[3:], far_clip[3:])
    mid, normed2 = norm_forward(place, inputs, shares, vectors)

    up, down = at.gather_feed_forward(w_up, w_down)
    positions = at.core * tokens + jnp.arange(tokens, dtype=jnp.int32)
    own_valid = (positions < lengths[0]).astype(F32)[:, None]
    grad_out = cotangent.astype(F32) * own_valid
    grad_branch = grad_out.astype(BF16)
    own_branch, far_branch = at.gather_tokens(grad_branch)

    own_normed2, far_normed2 = at.gather_tokens(normed2)
    own = feed_forward(place, own_normed2, own_branch, up, down, up_bias)
    far = feed_forward(place, far_normed2, far_branch, up, down, up_bias)
    shares = at.scatter_tokens(own[3:], far[3:])
    grad_mid, grad_attended, norm2_sums = norm_grads(
        place, grad_out, mid, shares, vectors, 5, True
    )
    moves, sizes = at.feed_forward_order(shard, hidden_width // dp)
    sorted_grads = feed_forward_grads(
        place,
        (own[0], far[0]),
        (own[1], far[1]),
        own_normed2 + far_normed2,
        own_branch + far_branch,
        moves,
        sizes,
    )
    by_rank, grad_w_down = at.scatter_feed_forward(sorted_grads, shard)
    grad_w_up = jnp.concatenate(by_rank, axis=1)
    out_shares = at.scatter_tokens(
        feed_forward_out(place, own[0], down), feed_forward_out(place, far[0], down)
    )
    branch = out_shares[0] + out_shares[1].astype(F32) + out_shares[2].astype(F32)
    output = (mid + branch + vectors[7:8]).astype(BF16)

    own_attended, far_attended = at.gather_tokens(grad_attended)
    own_back = attention_backward(
        place, 0, own_attended, own_inputs, own_clip[1], qkv, vectors, out_rows
    )
    far_back = attention_backward(
        place, 1, far_attended, far_inputs, far_clip[1], qkv, vectors, out_rows
    )
    shares = at.scatter_tokens(own_back[1:3], far_back[1:3])
    (input_grad,) = norm_grads(place, grad_mid, inputs, shares, vectors, 0, False)

    norm1_sums = own_back[3] + far_back[3]
    head_sums = own_back[4] + far_back[4]
    up_sums = (own[2] + far[2]).reshape(2 * dp // RANKS, extra - 8, shard // 2)
    up_sums = up_sums.transpose(1, 0, 2).reshape(extra - 8, rank_width)
    branch_sums = column_sums(grad_branch)
    nothing = jnp.zeros((2, width), F32)
    sums = jnp.concatenate(
        [norm1_sums, nothing, norm2_sums[2:], norm2_sums[:2], branch_sums, nothing, nothing]
    )
    nothing = jnp.zeros((4, rank_width), F32)
    rank_sums = jnp.concatenate(
        [
            nothing[:2],
            head_sums[:, :rank_width],
            head_sums[:, 2 * rank_width :],
            nothing,
            up_sums,
        ]
    )
    column_moves, column_sizes = at.column_order(shard)
    plane_moves, plane_sizes = at.plane_order(shard)
    sorted_grads = attention_grads(
        place,
        (own_clip[0], far_clip[0]),
        (own_back[0], far_back[0]),
        (own_clip[2], far_clip[2]),
        own_attended + far_attended,
        sums,
        rank_sums,
        (column_moves, plane_moves),
        (column_sizes, plane_sizes),
    )
    count = max(len(column_sizes), 1)
    by_rank = at.scatter_columns(sorted_grads[:count])
    grad_w_output = at.scatter_plane_rows(sorted_grads[count:])
    grad_w_query, grad_w_key, grad_w_value = (
        jnp.concatenate([part[:, i * rank_width : (i + 1) * rank_width] for part in by_rank], axis=1)
        for i in range(3)
    )
    sums = sum(part[:, 3 * rank_width :] for part in by_rank)
    shares = [sums[:, i] for i in range(8)] + [sums[:, 8:].T.reshape(-1)]
    return (
        output,
        input_grad,
        shares[0],
        shares[1],
        grad_w_query,
        shares[2],
        grad_w_key,
        grad_w_value,
        shares[3],
        grad_w_output,
        shares[4],
        shares[5],
        shares[6],
        grad_w_up,
        shares[8],
        grad_w_down,
        shares[7],
    )


def solution(mesh):
    rows, vector = P("dp", None), P("dp")
    own_rows, own_vector = P(AXES, None), P(AXES)
    return jax.shard_map(
        functools.partial(on_device, mesh.shape["dp"]),
        mesh=mesh,
        in_specs=(
            own_rows,
            vector,
            own_rows,
            vector,
            vector,
            rows,
            vector,
            rows,
            rows,
            vector,
            rows,
            vector,
            vector,
            vector,
            rows,
            vector,
            rows,
            vector,
        ),
        out_specs=(
            own_rows,
            own_rows,
            own_vector,
            own_vector,
            own_rows,
            own_vector,
            own_rows,
            own_rows,
            own_vector,
            own_rows,
            own_vector,
            own_vector,
            own_vector,
            own_rows,
            own_vector,
            own_rows,
            own_vector,
        ),
        check_vma=False,
    )
```

```python
import functools
import math

import jax
import jax.numpy as jnp
from jax import lax
from jax.experimental import pallas as pl
from jax.experimental.pallas import tpu as pltpu
from jax.sharding import PartitionSpec as P

HEAD = 80
EPS_NORM = 1e-05
MASKED = -1e30
RANKS = 4
AXES = ("dp", "seq")
BF16 = jnp.bfloat16
F32 = jnp.float32

CORE, ALONG_X, ALONG_Y, ALONG_Z, ALONG_Z2 = 1, 2, 4, 8, 16


def swap(values, mask, count):
    return lax.ppermute(values, AXES, [(place, place ^ mask) for place in range(count)])


def plane_route(planes):
    pairs = []
    for column in range(4):
        for plane in range(planes):
            for core in range(2):
                target_z = (plane >> 1) + 2 * core
                pairs.append(
                    (
                        (plane * 4 + column) * 2 + core,
                        (target_z * 4 + column) * 2 + (plane & 1),
                    )
                )
    return pairs


def move_blocks(arrays, moves, out_rows, place):
    columns = arrays[0].shape[1]

    def kernel(place_ref, *refs):
        in_refs, out_refs, sems = refs[: len(arrays)], refs[len(arrays) : -1], refs[-1]
        here = place_ref[0]
        copies = []
        for index, (array, source, out, target, rows) in enumerate(moves):
            source = pl.multiple_of(source(here), 8)
            target = pl.multiple_of(target(here), 8)
            copy = pltpu.make_async_copy(
                in_refs[array].at[pl.ds(source, rows)],
                out_refs[out].at[pl.ds(target, rows)],
                sems.at[index],
            )
            copy.start()
            copies.append(copy)
        for copy in copies:
            copy.wait()

    return pl.pallas_call(
        kernel,
        out_shape=[jax.ShapeDtypeStruct((rows, columns), arrays[0].dtype) for rows in out_rows],
        in_specs=[pl.BlockSpec(memory_space=pltpu.SMEM)]
        + [pl.BlockSpec(memory_space=pl.ANY)] * len(arrays),
        out_specs=[pl.BlockSpec(memory_space=pltpu.VMEM)] * len(out_rows),
        scratch_shapes=[pltpu.SemaphoreType.DMA((len(moves),))],
        compiler_params=pltpu.CompilerParams(vmem_limit_bytes=32 * 1024 * 1024),
    )(jnp.reshape(place, (1,)).astype(jnp.int32), *arrays)


def always(row):
    return lambda here: row


def xor_row(flip, rows, first=0, mask=15):
    return lambda here: jnp.bitwise_xor(jnp.bitwise_and(here, mask), flip) * rows + first


def tie(values, *others):
    return lax.optimization_barrier((values,) + others)[0]


def together(*values):
    return lax.optimization_barrier(values)


def rows_times(operand, weight):
    return lax.dot_general(operand, weight, (((1,), (0,)), ((), ())), preferred_element_type=F32)


def times_transposed(operand, weight):
    return lax.dot_general(operand, weight, (((1,), (1,)), ((), ())), preferred_element_type=F32)


def contract_rows(operand, other):
    return lax.dot_general(operand, other, (((0,), (0,)), ((), ())), preferred_element_type=F32)


def normalize(values):
    average = jnp.mean(values, axis=-1, keepdims=True)
    centred = values - average
    inverse = lax.rsqrt(jnp.mean(centred * centred, axis=-1, keepdims=True) + EPS_NORM)
    return (centred * inverse, inverse)


def norm_backward(grad_normed, normalized, inverse, norm_gain):
    scaled = grad_normed * norm_gain
    return inverse * (
        scaled
        - jnp.mean(scaled, axis=-1, keepdims=True)
        - normalized * jnp.mean(scaled * normalized, axis=-1, keepdims=True)
    )


def column_sums(values):
    return jnp.sum(values.astype(F32), axis=0, keepdims=True)


def local_call(kernel, outs, *operands, flops=0, scratch=(), limit=32):
    vmem = pl.BlockSpec(memory_space=pltpu.VMEM)
    shapes = [jax.ShapeDtypeStruct(shape, dtype) for shape, dtype in outs]
    moved = sum(math.prod(shape) * jnp.dtype(dtype).itemsize for shape, dtype in outs)
    moved += sum(operand.size * operand.dtype.itemsize for operand in operands)
    return pl.pallas_call(
        kernel,
        out_shape=shapes,
        in_specs=[pl.BlockSpec(memory_space=pltpu.SMEM)] + [vmem] * (len(operands) - 1),
        out_specs=[vmem] * len(outs),
        scratch_shapes=list(scratch),
        compiler_params=pltpu.CompilerParams(vmem_limit_bytes=limit * 1024 * 1024),
        cost_estimate=pl.CostEstimate(flops=flops * 20, bytes_accessed=moved * 20, transcendentals=0),
    )(*operands)


CHUNK = 64


def row_chunks(rows):
    return [slice(first, min(first + CHUNK, rows)) for first in range(0, rows, CHUNK)]


def head_slice(part, head, heads):
    first = (part * heads + head) * HEAD
    return slice(first, first + HEAD)


def cut_projections(place, projections, vectors):
    shard, width = projections[0].shape
    rank_width = width // RANKS
    extra = sum(vector.shape[0] for vector in vectors) // shard
    columns = 3 * rank_width + extra

    operands = (*projections, *vectors)

    def kernel(place_ref, *refs):
        sources, refs = refs[: len(operands)], refs[len(operands) :]
        same_ref, other_ref, blocks, rows = refs[:4]
        held, sems = refs[4:-1], refs[-1]
        copies = [
            pltpu.make_async_copy(source, target, sems.at[index])
            for index, (source, target) in enumerate(zip(sources, held))
        ]
        for copy in copies:
            copy.start()
        for copy in copies:
            copy.wait()
        projection_refs, vector_refs = held[:3], held[3:]
        row = 0
        for ref in vector_refs:
            values = ref[...].astype(F32)
            for first in range(0, ref.shape[0], shard):
                rows[row : row + 1, :] = values[first : first + shard].reshape(1, shard)
                row += 1
        turned = rows[...].T.astype(BF16)
        for rank in range(RANKS):
            cut = slice(rank * rank_width, (rank + 1) * rank_width)
            for part, ref in enumerate(projection_refs):
                blocks[rank, :, part * rank_width : (part + 1) * rank_width] = ref[:, cut]
            blocks[rank, :, 3 * rank_width :] = turned
        other_ref[...] = blocks[jnp.bitwise_xor(place_ref[1], 2)]
        same_ref[...] = blocks[place_ref[1]]

    return pl.pallas_call(
        kernel,
        out_shape=[jax.ShapeDtypeStruct((shard, columns), BF16)] * 2,
        in_specs=[pl.BlockSpec(memory_space=pltpu.SMEM)]
        + [pl.BlockSpec(memory_space=pl.ANY)] * len(operands),
        out_specs=[pl.BlockSpec(memory_space=pltpu.VMEM)] * 2,
        scratch_shapes=[
            pltpu.VMEM((RANKS, shard, columns), BF16),
            pltpu.VMEM((extra, shard), F32),
            *(pltpu.VMEM(operand.shape, operand.dtype) for operand in operands),
            pltpu.SemaphoreType.DMA((len(operands),)),
        ],
        compiler_params=pltpu.CompilerParams(vmem_limit_bytes=56 * 1024 * 1024),
    )(place, *operands)


def attention_forward(place, clip, inputs, qkv, vectors, out_rows):
    half, width = inputs[0].shape
    rows = 2 * half
    rank_width = width // RANKS
    heads = rank_width // HEAD
    scale = 1.0 / math.sqrt(HEAD)

    def kernel(
        place_ref,
        first_ref,
        second_ref,
        qkv_ref,
        vectors_ref,
        out_rows_ref,
        normed_ref,
        projected_ref,
        context_ref,
        kept_ref,
        sent_ref,
    ):
        core, rank, length = place_ref[0], place_ref[1], place_ref[2 + clip]
        gain, shift = vectors_ref[0:1, :], vectors_ref[1:2, :]
        for index, ref in enumerate((first_ref, second_ref)):
            for cut in row_chunks(half):
                normed = normalize(ref[cut, :].astype(F32))[0] * gain + shift
                normed_ref[index * half + cut.start : index * half + cut.stop, :] = normed.astype(
                    BF16
                )
        bias = jnp.zeros((1, rank_width), F32)
        value_bias = bias
        for other in range(RANKS):
            cut = slice(other * rank_width, (other + 1) * rank_width)
            bias += jnp.where(rank == other, vectors_ref[2:3, cut], 0.0)
            value_bias += jnp.where(rank == other, vectors_ref[3:4, cut], 0.0)
        biases = (bias, None, value_bias)
        projected = rows_times(normed_ref[...], qkv_ref[...])
        for part, added in enumerate(biases):
            values = projected[:, part * rank_width : (part + 1) * rank_width]
            values = values if added is None else values + added
            projected_ref[:, part * rank_width : (part + 1) * rank_width] = values.astype(BF16)
        positions = lax.broadcasted_iota(jnp.int32, (rows, rows), 1)
        positions = jnp.bitwise_and(positions + core * half, rows - 1)
        valid = positions < length
        for head in range(heads):
            queries = projected_ref[:, head_slice(0, head, heads)]
            keys = projected_ref[:, head_slice(1, head, heads)]
            values = projected_ref[:, head_slice(2, head, heads)]
            scores = jnp.where(valid, times_transposed(queries, keys) * scale, MASKED)
            weights = jnp.exp(scores - jnp.max(scores, axis=1, keepdims=True))
            weights = weights * (1.0 / jnp.sum(weights, axis=1, keepdims=True))
            context = rows_times(weights.astype(BF16), values)
            context_ref[:, head_slice(0, head, heads)] = context.astype(BF16)
        kept_ref[...] = rows_times(context_ref[0:half, :], out_rows_ref[...])
        sent_ref[...] = rows_times(context_ref[half:rows, :], out_rows_ref[...]).astype(BF16)

    return local_call(
        kernel,
        [
            ((rows, width), BF16),
            ((rows, 3 * rank_width), BF16),
            ((rows, rank_width), BF16),
            ((half, width), F32),
            ((half, width), BF16),
        ],
        place,
        *inputs,
        qkv,
        vectors,
        out_rows,
        flops=2 * rows * width * width + 4 * rows * rows * rank_width,
    )


def attention_backward(place, clip, grads, inputs, projected, qkv, vectors, out_rows):
    half, width = inputs[0].shape
    rows = 2 * half
    rank_width = width // RANKS
    heads = rank_width // HEAD
    scale = 1.0 / math.sqrt(HEAD)

    def kernel(
        place_ref,
        grad_first_ref,
        grad_second_ref,
        first_ref,
        second_ref,
        projected_ref,
        qkv_ref,
        vectors_ref,
        out_rows_ref,
        grads_ref,
        kept_ref,
        sent_ref,
        norm_sums_ref,
        head_sums_ref,
        context_ref,
        normed_ref,
    ):
        core, length = place_ref[0], place_ref[2 + clip]
        for index, ref in enumerate((grad_first_ref, grad_second_ref)):
            context_ref[index * half : (index + 1) * half, :] = times_transposed(
                ref[...], out_rows_ref[...]
            ).astype(BF16)
        positions = lax.broadcasted_iota(jnp.int32, (rows, rows), 0)
        positions = jnp.bitwise_and(positions + core * half, rows - 1)
        valid = positions < length
        for head in range(heads):
            queries = projected_ref[:, head_slice(0, head, heads)]
            keys = projected_ref[:, head_slice(1, head, heads)]
            values = projected_ref[:, head_slice(2, head, heads)]
            grad_context = context_ref[:, head_slice(0, head, heads)]
            scores = jnp.where(valid, times_transposed(keys, queries) * scale, MASKED)
            weights = jnp.exp(scores - jnp.max(scores, axis=0, keepdims=True))
            weights = weights * (1.0 / jnp.sum(weights, axis=0, keepdims=True))
            grad_weights = times_transposed(values, grad_context)
            inner = jnp.sum(weights * grad_weights, axis=0, keepdims=True)
            grad_scores = (weights * (grad_weights - inner)).astype(BF16)
            grad_query = contract_rows(grad_scores, keys) * scale
            grad_key = rows_times(grad_scores, queries) * scale
            grad_value = rows_times(weights.astype(BF16), grad_context)
            grads_ref[:, head_slice(0, head, heads)] = grad_query.astype(BF16)
            grads_ref[:, head_slice(1, head, heads)] = grad_key.astype(BF16)
            grads_ref[:, head_slice(2, head, heads)] = grad_value.astype(BF16)
        head_sums_ref[...] = column_sums(grads_ref[...])
        weight = qkv_ref[:, 0 : 3 * rank_width]
        gain_sum = jnp.zeros((1, width), F32)
        shift_sum = jnp.zeros((1, width), F32)
        for index, ref in enumerate((first_ref, second_ref)):
            normed_ref[...] = times_transposed(
                grads_ref[index * half : (index + 1) * half, :], weight
            )
            for cut in row_chunks(half):
                grad = normed_ref[cut, :]
                if index == 0:
                    kept_ref[cut, :] = grad
                else:
                    sent_ref[cut, :] = grad.astype(BF16)
                gain_sum += column_sums(grad * normalize(ref[cut, :].astype(F32))[0])
                shift_sum += column_sums(grad)
        norm_sums_ref[0:1, :] = gain_sum
        norm_sums_ref[1:2, :] = shift_sum

    return local_call(
        kernel,
        [
            ((rows, 3 * rank_width), BF16),
            ((half, width), F32),
            ((half, width), BF16),
            ((2, width), F32),
            ((1, 3 * rank_width), F32),
        ],
        place,
        *grads,
        *inputs,
        projected,
        qkv,
        vectors,
        out_rows,
        flops=2 * rows * width * width + 10 * rows * rows * rank_width,
        scratch=[pltpu.VMEM((rows, rank_width), BF16), pltpu.VMEM((half, width), F32)],
    )


def feed_forward(place, normed, branch, up, down, up_bias):
    half, width = normed[0].shape
    rows = 2 * half
    hidden_width = up.shape[1]
    chunk = 256

    def kernel(
        place_ref,
        first_ref,
        second_ref,
        branch_first_ref,
        branch_second_ref,
        up_ref,
        down_ref,
        bias_ref,
        hidden_ref,
        grad_ref,
        sums_ref,
        kept_ref,
        sent_ref,
    ):
        for begin in range(0, hidden_width, chunk):
            cut = slice(begin, begin + chunk)
            total = jnp.zeros((1, chunk), F32)
            for index, (ref, branch_ref) in enumerate(
                ((first_ref, branch_first_ref), (second_ref, branch_second_ref))
            ):
                here = slice(index * half, (index + 1) * half)
                pre = rows_times(ref[...], up_ref[:, cut]) + bias_ref[:, cut]
                grad_hidden = times_transposed(branch_ref[...], down_ref[cut, :])
                share = 0.5 * (1.0 + lax.erf(pre * math.sqrt(0.5)))
                hidden_ref[here, cut] = (pre * share).astype(BF16)
                slope = share + pre * (jnp.exp(-0.5 * pre * pre) * (1.0 / math.sqrt(2.0 * math.pi)))
                grad = (grad_hidden * slope).astype(BF16)
                grad_ref[here, cut] = grad
                total += column_sums(grad)
            sums_ref[:, cut] = total
        kept_ref[...] = times_transposed(grad_ref[0:half, :], up_ref[...])
        sent_ref[...] = times_transposed(grad_ref[half:rows, :], up_ref[...]).astype(BF16)

    return local_call(
        kernel,
        [
            ((rows, hidden_width), BF16),
            ((rows, hidden_width), BF16),
            ((1, hidden_width), F32),
            ((half, width), F32),
            ((half, width), BF16),
        ],
        place,
        *normed,
        *branch,
        up,
        down,
        up_bias,
        flops=6 * rows * width * hidden_width,
    )


def feed_forward_out(place, hidden, down):
    rows, width = hidden.shape[0], down.shape[1]
    half = rows // 2

    def kernel(place_ref, hidden_ref, down_ref, kept_ref, sent_ref):
        kept_ref[...] = rows_times(hidden_ref[0:half, :], down_ref[...])
        sent_ref[...] = rows_times(hidden_ref[half:rows, :], down_ref[...]).astype(BF16)

    return local_call(
        kernel,
        [((half, width), F32), ((half, width), BF16)],
        place,
        hidden,
        down,
        flops=2 * rows * hidden.shape[1] * width,
    )


def sort_rows(here, source_ref, out_refs, moves, array):
    for which, source, out, target, rows in moves:
        if which == array:
            first = pl.multiple_of(source(here), 16)
            out_refs[out][target(here) : target(here) + rows, :] = source_ref[pl.ds(first, rows), :]


def feed_forward_grads(place, hidden, grad_pre, normed, branch, moves, out_rows):
    half, width = normed[0].shape
    hidden_width = hidden[0].shape[1]

    def kernel(place_ref, *refs):
        hidden_refs, grad_refs = refs[0:2], refs[2:4]
        normed_refs, branch_refs = refs[4:8], refs[8:12]
        out_refs = refs[12:-2] if moves else refs[12:]
        up_ref, down_ref = refs[-2:] if moves else out_refs
        for target, lefts, rights in (
            (up_ref, normed_refs, grad_refs),
            (down_ref, hidden_refs, branch_refs),
        ):
            for begin in range(0, target.shape[0], 256):
                cut = slice(begin, begin + 256)
                total = 0.0
                for quarter in range(4):
                    rows = slice((quarter % 2) * half, (quarter % 2 + 1) * half)
                    if target is up_ref:
                        left, right = lefts[quarter][:, cut], rights[quarter // 2][rows, :]
                    else:
                        left, right = lefts[quarter // 2][rows, cut], rights[quarter][...]
                    total = total + contract_rows(left, right)
                target[cut, :] = total.astype(BF16)
        if moves:
            sort_rows(place_ref[4], up_ref, out_refs, moves, 0)
            sort_rows(place_ref[4], down_ref, out_refs, moves, 1)

    whole = [((width, hidden_width), BF16), ((hidden_width, width), BF16)]
    return local_call(
        kernel,
        [((rows, width), BF16) for rows in out_rows] if moves else whole,
        place,
        *hidden,
        *grad_pre,
        *normed,
        *branch,
        flops=16 * half * width * hidden_width,
        scratch=[pltpu.VMEM(shape, dtype) for shape, dtype in whole] if moves else [],
    )


def attention_grads(place, normed, grads, context, attended, sums, rank_sums, moves, out_rows):
    rows, width = normed[0].shape
    half = rows // 2
    rank_width = width // RANKS
    extra = sums.shape[0]
    columns = 3 * rank_width + extra
    column_moves, plane_moves = moves
    count = len(out_rows[0]) if column_moves else 1

    def kernel(place_ref, *refs):
        normed_refs, grad_refs, context_refs = refs[0:2], refs[2:4], refs[4:6]
        attended_refs, sums_ref, rank_ref = refs[6:10], refs[10], refs[11]
        outs = refs[12:-3] if column_moves else refs[12:-1]
        total_ref = refs[-1]
        rank = place_ref[1]
        target = refs[-3] if column_moves else outs[0]
        for begin in range(0, width, 256):
            cut = slice(begin, begin + 256)
            total = contract_rows(normed_refs[0][:, cut], grad_refs[0][...])
            total += contract_rows(normed_refs[1][:, cut], grad_refs[1][...])
            target[cut, 0 : 3 * rank_width] = total.astype(BF16)
        for other in range(RANKS):
            cut = slice(other * rank_width, (other + 1) * rank_width)
            total_ref[:, cut] = sums_ref[:, cut] + jnp.where(rank == other, rank_ref[...], 0.0)
        target[:, 3 * rank_width :] = total_ref[...].T.astype(BF16)
        total = 0.0
        for quarter in range(4):
            cut = slice((quarter % 2) * half, (quarter % 2 + 1) * half)
            total = total + contract_rows(
                context_refs[quarter // 2][cut, :], attended_refs[quarter][...]
            )
        plane_target = refs[-2] if column_moves else outs[1]
        plane_target[...] = total.astype(BF16)
        if column_moves:
            sort_rows(place_ref[4], target, outs[:count], column_moves, 0)
            sort_rows(place_ref[4], plane_target, outs[count:], plane_moves, 0)

    whole = [((width, columns), BF16), ((rank_width, width), BF16)]
    if column_moves:
        outs = [((rows_, columns), BF16) for rows_ in out_rows[0]]
        outs += [((rows_, width), BF16) for rows_ in out_rows[1]]
    else:
        outs = whole
    scratch = [pltpu.VMEM(shape, dtype) for shape, dtype in whole] if column_moves else []
    return local_call(
        kernel,
        outs,
        place,
        *normed,
        *grads,
        *context,
        *attended,
        sums,
        rank_sums,
        flops=4 * rows * width * columns + 4 * rows * rank_width * width,
        scratch=scratch + [pltpu.VMEM((extra, width), F32)],
    )


def norm_forward(place, inputs, shares, vectors):
    rows, width = inputs.shape

    def kernel(place_ref, inputs_ref, kept_ref, near_ref, far_ref, vectors_ref, mid_ref, normed_ref):
        for cut in row_chunks(rows):
            attended = kept_ref[cut, :] + near_ref[cut, :].astype(F32)
            attended += far_ref[cut, :].astype(F32)
            mid = inputs_ref[cut, :].astype(F32) + attended + vectors_ref[4:5, :]
            mid_ref[cut, :] = mid
            normed = normalize(mid)[0] * vectors_ref[5:6, :] + vectors_ref[6:7, :]
            normed_ref[cut, :] = normed.astype(BF16)

    return local_call(
        kernel, [((rows, width), F32), ((rows, width), BF16)], place, inputs, *shares, vectors
    )


def norm_grads(place, residual, values, shares, vectors, gain_row, with_sums):
    rows, width = residual.shape

    def kernel(
        place_ref, residual_ref, values_ref, kept_ref, near_ref, far_ref, vectors_ref, *out_refs
    ):
        totals = [jnp.zeros((1, width), F32)] * 3
        for cut in row_chunks(rows):
            grad = kept_ref[cut, :] + near_ref[cut, :].astype(F32)
            grad += far_ref[cut, :].astype(F32)
            normalized, inverse = normalize(values_ref[cut, :].astype(F32))
            gain = vectors_ref[gain_row : gain_row + 1, :]
            result = residual_ref[cut, :] + norm_backward(grad, normalized, inverse, gain)
            out_refs[0][cut, :] = result
            if with_sums:
                rounded = result.astype(BF16)
                out_refs[1][cut, :] = rounded
                terms = (grad * normalized, grad, rounded)
                totals = [total + column_sums(term) for total, term in zip(totals, terms)]
        if with_sums:
            for row, total in enumerate(totals):
                out_refs[2][row : row + 1, :] = total

    outs = [((rows, width), F32)]
    if with_sums:
        outs += [((rows, width), BF16), ((3, width), F32)]
    return local_call(kernel, outs, place, residual, values, *shares, vectors)


class Layout:
    def __init__(self, dp):
        self.dp = dp
        self.count = dp * 2
        self.planes = dp // 4
        self.direct = self.planes == 4
        self.dp_index = lax.axis_index("dp")
        self.core = lax.axis_index("seq")
        self.z = self.dp_index // 4
        self.y = (self.dp_index // 2) % 2
        self.x = self.dp_index % 2
        self.rank = (self.z % 2) * 2 + self.core

    def swap(self, values, mask):
        return swap(values, mask, self.count)

    def gather_tokens(self, values):
        across = self.swap(values, ALONG_Z)
        return (values, self.swap(values, CORE)), (across, self.swap(across, CORE))

    def scatter_tokens(self, own, far):
        crossing = (far[0] + self.swap(far[1], CORE).astype(F32)).astype(BF16)
        return own[0], self.swap(own[1], CORE), self.swap(crossing, ALONG_Z)

    def from_column(self, same, other):
        return (
            self.swap(other, ALONG_Z),
            self.swap(same, ALONG_Z2),
            self.swap(other, ALONG_Z | ALONG_Z2),
        )

    def spread_plane(self, first, second):
        first_x = self.swap(first, ALONG_X)
        second_y = self.swap(second, ALONG_Y)
        first_y = self.swap(jnp.concatenate([first, first_x]), ALONG_Y)
        second_x = self.swap(jnp.concatenate([second, second_y]), ALONG_X)
        return [first, first_x, first_y, second, second_y, second_x]

    def gather_columns(self, same, other):
        rows, columns = same.shape
        if not self.direct:
            return self.gather_columns_plainly(same, other)
        by_1, by_2, by_3 = self.from_column(same, other)
        spread = self.spread_plane(jnp.concatenate([same, by_2]), jnp.concatenate([by_1, by_3]))
        return move_blocks(
            spread, self.column_moves(rows, 2 * rows, 0), [self.dp * rows], self.dp_index
        )[0]

    def gather_columns_plainly(self, same, other):
        low = self.rank < 2
        both = jnp.stack([jnp.where(low, same, other), jnp.where(low, other, same)])
        whole = lax.all_gather(both, "dp", axis=0)
        mine = lax.dynamic_index_in_dim(whole, self.rank // 2, 1, keepdims=False)
        return mine.reshape(-1, same.shape[1])

    def column_moves(self, rows, stride, out):
        moves = []
        for far_z in range(2):
            first = far_z * rows
            for array, row, flip in (
                (0, first, 0),
                (1, first, 1),
                (2, first, 2),
                (2, stride + first, 3),
                (3, first, 4),
                (4, first, 6),
                (5, first, 5),
                (5, stride + first, 7),
            ):
                moves.append((array, always(row), out, xor_row(flip + 8 * far_z, rows), rows))
        return moves

    def gather_plane_rows(self, shard):
        rows, columns = shard.shape
        if not self.direct:
            whole = lax.all_gather(shard, "dp", axis=0, tiled=True)
            quarter = self.dp * rows // RANKS
            return lax.dynamic_slice_in_dim(whole, self.rank * quarter, quarter, 0)
        mine = lax.ppermute(shard, AXES, plane_route(self.planes))
        by_x = self.swap(mine, ALONG_X)
        by_y = self.swap(jnp.concatenate([mine, by_x]), ALONG_Y)
        sources = ((0, 0, 0), (1, 0, 1), (2, 0, 2), (2, rows, 3))
        moves = [
            (array, always(row), 0, xor_row(flip, rows, 0, 3), rows) for array, row, flip in sources
        ]
        return move_blocks([mine, by_x, by_y], moves, [4 * rows], self.dp_index)[0]

    def gather_feed_forward(self, w_up, w_down):
        shard, hidden = w_up.shape
        columns = hidden // RANKS
        rows, width = w_down.shape
        same = lax.dynamic_slice_in_dim(w_up, self.rank * columns, columns, 1)
        other = lax.dynamic_slice_in_dim(w_up, (self.rank ^ 2) * columns, columns, 1)
        if not self.direct:
            return self.gather_columns_plainly(same, other), self.gather_plane_rows(w_down)
        by_1, by_2, by_3 = self.from_column(same, other)
        mine = lax.ppermute(w_down, AXES, plane_route(self.planes))
        half = rows // 2
        first = jnp.concatenate([same, by_2, mine[:half]])
        second = jnp.concatenate([by_1, by_3, mine[half:]])
        spread = self.spread_plane(first, second)
        stride = 2 * shard + half
        moves = self.column_moves(shard, stride, 0)
        for array, row, flip, upper in (
            (0, 0, 0, 0),
            (1, 0, 1, 0),
            (2, 0, 2, 0),
            (2, stride, 3, 0),
            (3, 0, 0, 1),
            (4, 0, 2, 1),
            (5, 0, 1, 1),
            (5, stride, 3, 1),
        ):
            source = always(row + 2 * shard)
            moves.append((array, source, 1, xor_row(flip, rows, upper * half, 3), half))
        return move_blocks(spread, moves, [self.dp * shard, 4 * rows], self.dp_index)

    def sum_first(self, kept, received):
        both = kept.astype(F32) + received.astype(F32)
        rows = both.shape[0] // 2
        return both[:rows], both[rows:].astype(BF16)

    def across_column(self, first, second, rows):
        blocks = jnp.stack([first[:rows], second[:rows], first[rows : 2 * rows], second[rows : 2 * rows]])
        blocks = blocks.reshape(4, 2, rows // 2, first.shape[1])
        mine = lax.dynamic_index_in_dim(blocks, self.core, 1, keepdims=False)
        away = lax.dynamic_index_in_dim(blocks, 1 - self.core, 1, keepdims=False).astype(BF16)
        both = jnp.stack([mine.astype(BF16), self.swap(away, CORE)], axis=1)
        return both[0], [self.swap(both[step], step * ALONG_Z) for step in range(1, 4)]

    def sum_column(self, both, by):
        near = both.astype(F32) + by[1].astype(F32)
        far = by[0].astype(F32) + by[2].astype(F32)
        return self.in_rank_order([near[0], near[1], far[0], far[1]])

    def in_rank_order(self, ranks):
        high, low = self.rank // 2 == 1, self.rank % 2 == 1
        ranks = [jnp.where(low, ranks[i ^ 1], ranks[i]) for i in range(4)]
        return [jnp.where(high, ranks[i ^ 2], ranks[i]) for i in range(4)]

    def column_parts(self, rows, extra, array):
        moves = []
        half = 2 * rows + extra
        for out, flips in enumerate(((0, 1), (2, 3), (4, 6), (5, 7))):
            for block, flip in enumerate(flips):
                for far_z in range(2):
                    target = block * half + far_z * rows
                    moves.append(
                        (array, xor_row(flip + 8 * far_z, rows), out, always(target), rows)
                    )
        return moves

    def column_order(self, rows):
        return (self.column_parts(rows, 0, 0), [4 * rows] * 4) if self.direct else ([], [])

    def scatter_columns_plainly(self, grads):
        dp, rows, columns = self.dp, grads.shape[0] // self.dp, grads.shape[1]
        whole = jnp.zeros((dp * rows, RANKS, columns), BF16)
        whole = lax.dynamic_update_slice_in_dim(whole, grads[:, None, :], self.rank, 1)
        mine = lax.psum_scatter(
            whole.reshape(dp * rows, RANKS * columns).astype(F32),
            AXES,
            scatter_dimension=0,
            tiled=True,
        )
        return [mine[:, rank * columns : (rank + 1) * columns] for rank in range(RANKS)]

    def plane_order(self, rows):
        if not self.direct:
            return [], []
        moves = [
            (0, xor_row(flip, rows, 0, 3), flip // 2, always(flip % 2 * rows), rows)
            for flip in range(4)
        ]
        return moves, [2 * rows] * 2

    def scatter_plane_rows_plainly(self, grads):
        rows, columns = grads.shape
        whole = jnp.zeros((RANKS, rows, columns), BF16)
        whole = lax.dynamic_update_slice_in_dim(whole, grads[None], self.rank, 0)
        return lax.psum_scatter(
            whole.reshape(RANKS * rows, columns).astype(F32),
            AXES,
            scatter_dimension=0,
            tiled=True,
        )

    def to_owners(self, lower, upper):
        back = [(target, source) for source, target in plane_route(self.planes)]
        crossed = [(source, target ^ CORE) for source, target in back]
        high = self.z // 2 == 1
        straight = jnp.where(high, upper, lower).astype(BF16)
        other = jnp.where(high, lower, upper).astype(BF16)
        return lax.ppermute(straight, AXES, back), lax.ppermute(other, AXES, crossed)

    def feed_forward_order(self, shard, rows):
        if not self.direct:
            return [], []
        half = rows // 2
        stride = 2 * shard + half
        moves = self.column_parts(shard, half, 0)
        for out, (flips, upper) in enumerate((((0, 1), 0), ((2, 3), 0), ((0, 2), 1), ((1, 3), 1))):
            for block, flip in enumerate(flips):
                target = always(block * stride + 2 * shard)
                moves.append((1, xor_row(flip, rows, upper * half, 3), out, target, half))
        return moves, [2 * stride] * 4


def on_device(
    dp,
    inputs,
    lengths,
    cotangent,
    norm1_gain,
    norm1_shift,
    w_query,
    b_query,
    w_key,
    w_value,
    b_value,
    w_output,
    b_output,
    norm2_gain,
    norm2_shift,
    w_up,
    b_up,
    w_down,
    b_down,
):
    at = Layout(dp)
    tokens, width = inputs.shape
    shard = w_query.shape[0]
    hidden_width = w_up.shape[1]
    rank_width = width // RANKS
    rank_hidden = hidden_width // RANKS

    partner_length = at.swap(lengths, ALONG_Z)
    place = jnp.stack([at.core, at.rank, lengths[0], partner_length[0], at.dp_index])
    place = place.astype(jnp.int32)
    here = jnp.stack([at.core, at.rank]).astype(jnp.int32)

    vectors = [norm1_gain, norm1_shift, b_query, b_value, b_output, norm2_gain, norm2_shift, b_down]
    extra = len(vectors) + b_up.shape[0] // shard
    same, other = cut_projections(here, (w_query, w_key, w_value), (*vectors, b_up))
    own_inputs, far_inputs = at.gather_tokens(inputs)
    qkv = at.gather_columns(same, other)
    vectors = qkv[:, 3 * rank_width :].astype(F32).T
    up_bias = vectors[8:].reshape(extra - 8, dp, shard).transpose(1, 0, 2).reshape(1, hidden_width)
    up_bias = lax.dynamic_slice_in_dim(up_bias, at.rank * rank_hidden, rank_hidden, 1)
    out_rows = at.gather_plane_rows(w_output)

    far_clip = attention_forward(place, 1, far_inputs, qkv, vectors, out_rows)
    own_clip = attention_forward(place, 0, own_inputs, qkv, vectors, out_rows)
    shares = at.scatter_tokens(own_clip[3:], far_clip[3:])
    mid, normed2 = norm_forward(place, inputs, shares, vectors)

    up, down = at.gather_feed_forward(w_up, w_down)
    positions = at.core * tokens + jnp.arange(tokens, dtype=jnp.int32)
    own_valid = (positions < lengths[0]).astype(F32)[:, None]
    grad_out = cotangent.astype(F32) * own_valid
    grad_branch = grad_out.astype(BF16)
    own_branch, far_branch = at.gather_tokens(grad_branch)

    own_normed2, far_normed2 = at.gather_tokens(normed2)
    own = feed_forward(place, own_normed2, own_branch, up, down, up_bias)
    far = feed_forward(place, far_normed2, far_branch, up, down, up_bias)
    shares = at.scatter_tokens(own[3:], far[3:])
    grad_mid, grad_attended, norm2_sums = norm_grads(
        place, grad_out, mid, shares, vectors, 5, True
    )
    moves, sizes = at.feed_forward_order(shard, hidden_width // dp)
    sorted_grads = feed_forward_grads(
        place,
        (own[0], far[0]),
        (own[1], far[1]),
        own_normed2 + far_normed2,
        own_branch + far_branch,
        moves,
        sizes,
    )
    own_out, far_out = feed_forward_out(place, own[0], down), feed_forward_out(place, far[0], down)
    out_near = at.swap(own_out[1], CORE)
    out_crossing = (far_out[0] + at.swap(far_out[1], CORE).astype(F32)).astype(BF16)

    across = at.swap(grad_attended, ALONG_Z)
    own_attended = (grad_attended, at.swap(grad_attended, CORE))
    own_back = attention_backward(
        place, 0, own_attended, own_inputs, own_clip[1], qkv, vectors, out_rows
    )
    across = tie(across, own_back[2])
    far_attended = (across, at.swap(across, CORE))
    out_far = at.swap(tie(out_crossing, across), ALONG_Z)
    far_back = attention_backward(
        place, 1, far_attended, far_inputs, far_clip[1], qkv, vectors, out_rows
    )

    if at.direct:
        kept_1, sent_1, kept_2, sent_2 = sorted_grads
        up_first = at.sum_first(tie(kept_1, own_back[2]), at.swap(sent_1, ALONG_Y))
        up_second = at.sum_first(tie(kept_2, own_back[2]), at.swap(sent_2, ALONG_X))
        up_received = at.swap(up_first[1], ALONG_X), at.swap(up_second[1], ALONG_Y)
    else:
        grad_w_up = at.scatter_columns_plainly(sorted_grads[0])
        grad_w_down = at.scatter_plane_rows_plainly(sorted_grads[1])

    norm1_sums = own_back[3] + far_back[3]
    head_sums = own_back[4] + far_back[4]
    up_sums = (own[2] + far[2]).reshape(2 * dp // RANKS, extra - 8, shard // 2)
    up_sums = up_sums.transpose(1, 0, 2).reshape(extra - 8, rank_width)
    branch_sums = column_sums(grad_branch)
    nothing = jnp.zeros((2, width), F32)
    sums = jnp.concatenate(
        [norm1_sums, nothing, norm2_sums[2:], norm2_sums[:2], branch_sums, nothing, nothing]
    )
    nothing = jnp.zeros((4, rank_width), F32)
    rank_sums = jnp.concatenate(
        [
            nothing[:2],
            head_sums[:, :rank_width],
            head_sums[:, 2 * rank_width :],
            nothing,
            up_sums,
        ]
    )
    column_moves, column_sizes = at.column_order(shard)
    plane_moves, plane_sizes = at.plane_order(shard)
    sorted_grads = attention_grads(
        place,
        (own_clip[0], far_clip[0]),
        (own_back[0], far_back[0]),
        (own_clip[2], far_clip[2]),
        own_attended + far_attended,
        sums,
        rank_sums,
        (column_moves, plane_moves),
        (column_sizes, plane_sizes),
    )
    back_near = at.swap(own_back[2], CORE)
    back_crossing = (far_back[1] + at.swap(far_back[2], CORE).astype(F32)).astype(BF16)
    if at.direct:
        half = shard // 2
        *sorted_grads, out_far, back_far, received_1, received_2 = together(
            *sorted_grads, out_far, at.swap(back_crossing, ALONG_Z), *up_received
        )
        kept_1, sent_1, kept_2, sent_2, output_kept, output_sent = sorted_grads
        first, second = up_first[0] + received_1.astype(F32), up_second[0] + received_2.astype(F32)
        up_both, up_by = at.across_column(first, second, shard)
        received_1, received_2, output_sent, *up_by = together(
            at.swap(sent_1, ALONG_Y), at.swap(sent_2, ALONG_X), output_sent, *up_by
        )
        qkv_first, qkv_second = at.sum_first(kept_1, received_1), at.sum_first(kept_2, received_2)
        received_1, received_2, output_sent, *owners = together(
            at.swap(qkv_first[1], ALONG_X),
            at.swap(qkv_second[1], ALONG_Y),
            at.swap(output_sent, ALONG_Y),
            *at.to_owners(first[2 * shard :], second[2 * shard :]),
        )
        grad_w_down = owners[0].astype(F32) + owners[1].astype(F32)
        grad_w_up = at.sum_column(up_both, up_by)
        first = qkv_first[0] + received_1.astype(F32)
        second = qkv_second[0] + received_2.astype(F32)
        output_first = at.sum_first(output_kept, output_sent)
        grad_output = output_first[0] + at.swap(output_first[1], ALONG_X).astype(F32)
        both, by = at.across_column(first, second, shard)
        *by, lower, upper = together(*by, *at.to_owners(grad_output[:half], grad_output[half:]))
        by_rank = at.sum_column(both, by)
        grad_w_output = lower.astype(F32) + upper.astype(F32)
    else:
        back_far = at.swap(back_crossing, ALONG_Z)
        by_rank = at.scatter_columns_plainly(sorted_grads[0])
        grad_w_output = at.scatter_plane_rows_plainly(sorted_grads[1])
    shares = (own_back[1], back_near, back_far)
    (input_grad,) = norm_grads(place, grad_mid, inputs, shares, vectors, 0, False)
    grad_w_up = jnp.concatenate(grad_w_up, axis=1)
    branch = own_out[0] + out_near.astype(F32) + out_far.astype(F32)
    output = (mid + branch + vectors[7:8]).astype(BF16)
    grad_w_query, grad_w_key, grad_w_value = (
        jnp.concatenate([part[:, i * rank_width : (i + 1) * rank_width] for part in by_rank], axis=1)
        for i in range(3)
    )
    sums = sum(part[:, 3 * rank_width :] for part in by_rank)
    shares = [sums[:, i] for i in range(8)] + [sums[:, 8:].T.reshape(-1)]
    return (
        output,
        input_grad,
        shares[0],
        shares[1],
        grad_w_query,
        shares[2],
        grad_w_key,
        grad_w_value,
        shares[3],
        grad_w_output,
        shares[4],
        shares[5],
        shares[6],
        grad_w_up,
        shares[8],
        grad_w_down,
        shares[7],
    )


def solution(mesh):
    rows, vector = P("dp", None), P("dp")
    own_rows, own_vector = P(AXES, None), P(AXES)
    return jax.shard_map(
        functools.partial(on_device, mesh.shape["dp"]),
        mesh=mesh,
        in_specs=(
            own_rows,
            vector,
            own_rows,
            vector,
            vector,
            rows,
            vector,
            rows,
            rows,
            vector,
            rows,
            vector,
            vector,
            vector,
            rows,
            vector,
            rows,
            vector,
        ),
        out_specs=(
            own_rows,
            own_rows,
            own_vector,
            own_vector,
            own_rows,
            own_vector,
            own_rows,
            own_rows,
            own_vector,
            own_rows,
            own_vector,
            own_vector,
            own_vector,
            own_rows,
            own_vector,
            own_rows,
            own_vector,
        ),
        check_vma=False,
    )
```

```python
import functools
import math

import jax
import jax.numpy as jnp
from jax import lax
from jax.experimental import pallas as pl
from jax.experimental.pallas import tpu as pltpu
from jax.sharding import PartitionSpec as P

HEAD = 80
EPS_NORM = 1e-05
MASKED = -1e30
RANKS = 4
AXES = ("dp", "seq")
BF16 = jnp.bfloat16
F32 = jnp.float32

CORE, ALONG_X, ALONG_Y, ALONG_Z, ALONG_Z2 = 1, 2, 4, 8, 16


def swap(values, mask, count):
    return lax.ppermute(values, AXES, [(place, place ^ mask) for place in range(count)])


def plane_route(planes):
    pairs = []
    for column in range(4):
        for plane in range(planes):
            for core in range(2):
                target_z = (plane >> 1) + 2 * core
                pairs.append(
                    (
                        (plane * 4 + column) * 2 + core,
                        (target_z * 4 + column) * 2 + (plane & 1),
                    )
                )
    return pairs


def move_blocks(arrays, moves, out_rows, place):
    columns = arrays[0].shape[1]

    def kernel(place_ref, *refs):
        in_refs, out_refs, sems = refs[: len(arrays)], refs[len(arrays) : -1], refs[-1]
        here = place_ref[0]
        copies = []
        for index, (array, source, out, target, rows) in enumerate(moves):
            source = pl.multiple_of(source(here), 8)
            target = pl.multiple_of(target(here), 8)
            copy = pltpu.make_async_copy(
                in_refs[array].at[pl.ds(source, rows)],
                out_refs[out].at[pl.ds(target, rows)],
                sems.at[index],
            )
            copy.start()
            copies.append(copy)
        for copy in copies:
            copy.wait()

    return pl.pallas_call(
        kernel,
        out_shape=[jax.ShapeDtypeStruct((rows, columns), arrays[0].dtype) for rows in out_rows],
        in_specs=[pl.BlockSpec(memory_space=pltpu.SMEM)]
        + [pl.BlockSpec(memory_space=pl.ANY)] * len(arrays),
        out_specs=[pl.BlockSpec(memory_space=pltpu.VMEM)] * len(out_rows),
        scratch_shapes=[pltpu.SemaphoreType.DMA((len(moves),))],
        compiler_params=pltpu.CompilerParams(vmem_limit_bytes=32 * 1024 * 1024),
    )(jnp.reshape(place, (1,)).astype(jnp.int32), *arrays)


def always(row):
    return lambda here: row


def xor_row(flip, rows, first=0, mask=15):
    return lambda here: jnp.bitwise_xor(jnp.bitwise_and(here, mask), flip) * rows + first


def tie(values, *others):
    return lax.optimization_barrier((values,) + others)[0]


def together(*values):
    return lax.optimization_barrier(values)


def rows_times(operand, weight):
    return lax.dot_general(operand, weight, (((1,), (0,)), ((), ())), preferred_element_type=F32)


def times_transposed(operand, weight):
    return lax.dot_general(operand, weight, (((1,), (1,)), ((), ())), preferred_element_type=F32)


def contract_rows(operand, other):
    return lax.dot_general(operand, other, (((0,), (0,)), ((), ())), preferred_element_type=F32)


def normalize(values):
    average = jnp.mean(values, axis=-1, keepdims=True)
    centred = values - average
    inverse = lax.rsqrt(jnp.mean(centred * centred, axis=-1, keepdims=True) + EPS_NORM)
    return (centred * inverse, inverse)


def norm_backward(grad_normed, normalized, inverse, norm_gain):
    scaled = grad_normed * norm_gain
    return inverse * (
        scaled
        - jnp.mean(scaled, axis=-1, keepdims=True)
        - normalized * jnp.mean(scaled * normalized, axis=-1, keepdims=True)
    )


def column_sums(values):
    return jnp.sum(values.astype(F32), axis=0, keepdims=True)


def local_call(kernel, outs, *operands, flops=0, scratch=(), limit=32):
    vmem = pl.BlockSpec(memory_space=pltpu.VMEM)
    shapes = [jax.ShapeDtypeStruct(shape, dtype) for shape, dtype in outs]
    moved = sum(math.prod(shape) * jnp.dtype(dtype).itemsize for shape, dtype in outs)
    moved += sum(operand.size * operand.dtype.itemsize for operand in operands)
    return pl.pallas_call(
        kernel,
        out_shape=shapes,
        in_specs=[pl.BlockSpec(memory_space=pltpu.SMEM)] + [vmem] * (len(operands) - 1),
        out_specs=[vmem] * len(outs),
        scratch_shapes=list(scratch),
        compiler_params=pltpu.CompilerParams(vmem_limit_bytes=limit * 1024 * 1024),
        cost_estimate=pl.CostEstimate(flops=flops * 20, bytes_accessed=moved * 20, transcendentals=0),
    )(*operands)


CHUNK = 64


def row_chunks(rows):
    return [slice(first, min(first + CHUNK, rows)) for first in range(0, rows, CHUNK)]


def head_slice(part, head, heads):
    first = (part * heads + head) * HEAD
    return slice(first, first + HEAD)


def cut_projections(place, projections, vectors):
    shard, width = projections[0].shape
    rank_width = width // RANKS
    extra = sum(vector.shape[0] for vector in vectors) // shard
    columns = 3 * rank_width + extra

    operands = (*projections, *vectors)

    def kernel(place_ref, *refs):
        sources, refs = refs[: len(operands)], refs[len(operands) :]
        same_ref, other_ref, blocks, rows = refs[:4]
        held, sems = refs[4:-1], refs[-1]
        copies = [
            pltpu.make_async_copy(source, target, sems.at[index])
            for index, (source, target) in enumerate(zip(sources, held))
        ]
        for copy in copies:
            copy.start()
        for copy in copies:
            copy.wait()
        projection_refs, vector_refs = held[:3], held[3:]
        row = 0
        for ref in vector_refs:
            values = ref[...].astype(F32)
            for first in range(0, ref.shape[0], shard):
                rows[row : row + 1, :] = values[first : first + shard].reshape(1, shard)
                row += 1
        turned = rows[...].T.astype(BF16)
        for rank in range(RANKS):
            cut = slice(rank * rank_width, (rank + 1) * rank_width)
            for part, ref in enumerate(projection_refs):
                blocks[rank, :, part * rank_width : (part + 1) * rank_width] = ref[:, cut]
            blocks[rank, :, 3 * rank_width :] = turned
        other_ref[...] = blocks[jnp.bitwise_xor(place_ref[1], 2)]
        same_ref[...] = blocks[place_ref[1]]

    return pl.pallas_call(
        kernel,
        out_shape=[jax.ShapeDtypeStruct((shard, columns), BF16)] * 2,
        in_specs=[pl.BlockSpec(memory_space=pltpu.SMEM)]
        + [pl.BlockSpec(memory_space=pl.ANY)] * len(operands),
        out_specs=[pl.BlockSpec(memory_space=pltpu.VMEM)] * 2,
        scratch_shapes=[
            pltpu.VMEM((RANKS, shard, columns), BF16),
            pltpu.VMEM((extra, shard), F32),
            *(pltpu.VMEM(operand.shape, operand.dtype) for operand in operands),
            pltpu.SemaphoreType.DMA((len(operands),)),
        ],
        compiler_params=pltpu.CompilerParams(vmem_limit_bytes=56 * 1024 * 1024),
    )(place, *operands)


def attention_forward(place, clip, inputs, qkv, vectors, out_rows):
    half, width = inputs[0].shape
    rows = 2 * half
    rank_width = width // RANKS
    heads = rank_width // HEAD
    scale = 1.0 / math.sqrt(HEAD)

    def kernel(
        place_ref,
        first_ref,
        second_ref,
        qkv_ref,
        vectors_ref,
        out_rows_ref,
        normed_ref,
        projected_ref,
        context_ref,
        kept_ref,
        sent_ref,
    ):
        core, rank, length = place_ref[0], place_ref[1], place_ref[2 + clip]
        gain, shift = vectors_ref[0:1, :], vectors_ref[1:2, :]
        for index, ref in enumerate((first_ref, second_ref)):
            for cut in row_chunks(half):
                normed = normalize(ref[cut, :].astype(F32))[0] * gain + shift
                normed_ref[index * half + cut.start : index * half + cut.stop, :] = normed.astype(
                    BF16
                )
        bias = jnp.zeros((1, rank_width), F32)
        value_bias = bias
        for other in range(RANKS):
            cut = slice(other * rank_width, (other + 1) * rank_width)
            bias += jnp.where(rank == other, vectors_ref[2:3, cut], 0.0)
            value_bias += jnp.where(rank == other, vectors_ref[3:4, cut], 0.0)
        biases = (bias, None, value_bias)
        projected = rows_times(normed_ref[...], qkv_ref[...])
        for part, added in enumerate(biases):
            values = projected[:, part * rank_width : (part + 1) * rank_width]
            values = values if added is None else values + added
            projected_ref[:, part * rank_width : (part + 1) * rank_width] = values.astype(BF16)
        positions = lax.broadcasted_iota(jnp.int32, (rows, rows), 1)
        positions = jnp.bitwise_and(positions + core * half, rows - 1)
        valid = positions < length
        for head in range(heads):
            queries = projected_ref[:, head_slice(0, head, heads)]
            keys = projected_ref[:, head_slice(1, head, heads)]
            values = projected_ref[:, head_slice(2, head, heads)]
            scores = jnp.where(valid, times_transposed(queries, keys) * scale, MASKED)
            weights = jnp.exp(scores - jnp.max(scores, axis=1, keepdims=True))
            weights = weights * (1.0 / jnp.sum(weights, axis=1, keepdims=True))
            context = rows_times(weights.astype(BF16), values)
            context_ref[:, head_slice(0, head, heads)] = context.astype(BF16)
        kept_ref[...] = rows_times(context_ref[0:half, :], out_rows_ref[...])
        sent_ref[...] = rows_times(context_ref[half:rows, :], out_rows_ref[...]).astype(BF16)

    return local_call(
        kernel,
        [
            ((rows, width), BF16),
            ((rows, 3 * rank_width), BF16),
            ((rows, rank_width), BF16),
            ((half, width), F32),
            ((half, width), BF16),
        ],
        place,
        *inputs,
        qkv,
        vectors,
        out_rows,
        flops=2 * rows * width * width + 4 * rows * rows * rank_width,
    )


def attention_backward(place, clip, grads, inputs, projected, qkv, vectors, out_rows):
    half, width = inputs[0].shape
    rows = 2 * half
    rank_width = width // RANKS
    heads = rank_width // HEAD
    scale = 1.0 / math.sqrt(HEAD)

    def kernel(
        place_ref,
        grad_first_ref,
        grad_second_ref,
        first_ref,
        second_ref,
        projected_ref,
        qkv_ref,
        vectors_ref,
        out_rows_ref,
        grads_ref,
        kept_ref,
        sent_ref,
        norm_sums_ref,
        head_sums_ref,
        context_ref,
        normed_ref,
    ):
        core, length = place_ref[0], place_ref[2 + clip]
        for index, ref in enumerate((grad_first_ref, grad_second_ref)):
            context_ref[index * half : (index + 1) * half, :] = times_transposed(
                ref[...], out_rows_ref[...]
            ).astype(BF16)
        positions = lax.broadcasted_iota(jnp.int32, (rows, rows), 0)
        positions = jnp.bitwise_and(positions + core * half, rows - 1)
        valid = positions < length
        for head in range(heads):
            queries = projected_ref[:, head_slice(0, head, heads)]
            keys = projected_ref[:, head_slice(1, head, heads)]
            values = projected_ref[:, head_slice(2, head, heads)]
            grad_context = context_ref[:, head_slice(0, head, heads)]
            scores = jnp.where(valid, times_transposed(keys, queries) * scale, MASKED)
            weights = jnp.exp(scores - jnp.max(scores, axis=0, keepdims=True))
            weights = weights * (1.0 / jnp.sum(weights, axis=0, keepdims=True))
            grad_weights = times_transposed(values, grad_context)
            inner = jnp.sum(weights * grad_weights, axis=0, keepdims=True)
            grad_scores = (weights * (grad_weights - inner)).astype(BF16)
            grad_query = contract_rows(grad_scores, keys) * scale
            grad_key = rows_times(grad_scores, queries) * scale
            grad_value = rows_times(weights.astype(BF16), grad_context)
            grads_ref[:, head_slice(0, head, heads)] = grad_query.astype(BF16)
            grads_ref[:, head_slice(1, head, heads)] = grad_key.astype(BF16)
            grads_ref[:, head_slice(2, head, heads)] = grad_value.astype(BF16)
        head_sums_ref[...] = column_sums(grads_ref[...])
        weight = qkv_ref[:, 0 : 3 * rank_width]
        gain_sum = jnp.zeros((1, width), F32)
        shift_sum = jnp.zeros((1, width), F32)
        for index, ref in enumerate((first_ref, second_ref)):
            normed_ref[...] = times_transposed(
                grads_ref[index * half : (index + 1) * half, :], weight
            )
            for cut in row_chunks(half):
                grad = normed_ref[cut, :]
                if index == 0:
                    kept_ref[cut, :] = grad
                else:
                    sent_ref[cut, :] = grad.astype(BF16)
                gain_sum += column_sums(grad * normalize(ref[cut, :].astype(F32))[0])
                shift_sum += column_sums(grad)
        norm_sums_ref[0:1, :] = gain_sum
        norm_sums_ref[1:2, :] = shift_sum

    return local_call(
        kernel,
        [
            ((rows, 3 * rank_width), BF16),
            ((half, width), F32),
            ((half, width), BF16),
            ((2, width), F32),
            ((1, 3 * rank_width), F32),
        ],
        place,
        *grads,
        *inputs,
        projected,
        qkv,
        vectors,
        out_rows,
        flops=2 * rows * width * width + 10 * rows * rows * rank_width,
        scratch=[pltpu.VMEM((rows, rank_width), BF16), pltpu.VMEM((half, width), F32)],
    )


def feed_forward(place, normed, branch, up, down, up_bias):
    half, width = normed[0].shape
    rows = 2 * half
    hidden_width = up.shape[1]
    chunk = 256

    def kernel(
        place_ref,
        first_ref,
        second_ref,
        branch_first_ref,
        branch_second_ref,
        up_ref,
        down_ref,
        bias_ref,
        hidden_ref,
        grad_ref,
        sums_ref,
        kept_ref,
        sent_ref,
    ):
        for begin in range(0, hidden_width, chunk):
            cut = slice(begin, begin + chunk)
            total = jnp.zeros((1, chunk), F32)
            for index, (ref, branch_ref) in enumerate(
                ((first_ref, branch_first_ref), (second_ref, branch_second_ref))
            ):
                here = slice(index * half, (index + 1) * half)
                pre = rows_times(ref[...], up_ref[:, cut]) + bias_ref[:, cut]
                grad_hidden = times_transposed(branch_ref[...], down_ref[cut, :])
                share = 0.5 * (1.0 + lax.erf(pre * math.sqrt(0.5)))
                hidden_ref[here, cut] = (pre * share).astype(BF16)
                slope = share + pre * (jnp.exp(-0.5 * pre * pre) * (1.0 / math.sqrt(2.0 * math.pi)))
                grad = (grad_hidden * slope).astype(BF16)
                grad_ref[here, cut] = grad
                total += column_sums(grad)
            sums_ref[:, cut] = total
        kept_ref[...] = times_transposed(grad_ref[0:half, :], up_ref[...])
        sent_ref[...] = times_transposed(grad_ref[half:rows, :], up_ref[...]).astype(BF16)

    return local_call(
        kernel,
        [
            ((rows, hidden_width), BF16),
            ((rows, hidden_width), BF16),
            ((1, hidden_width), F32),
            ((half, width), F32),
            ((half, width), BF16),
        ],
        place,
        *normed,
        *branch,
        up,
        down,
        up_bias,
        flops=6 * rows * width * hidden_width,
    )


def feed_forward_out(place, hidden, down):
    rows, width = hidden.shape[0], down.shape[1]
    half = rows // 2

    def kernel(place_ref, hidden_ref, down_ref, kept_ref, sent_ref):
        kept_ref[...] = rows_times(hidden_ref[0:half, :], down_ref[...])
        sent_ref[...] = rows_times(hidden_ref[half:rows, :], down_ref[...]).astype(BF16)

    return local_call(
        kernel,
        [((half, width), F32), ((half, width), BF16)],
        place,
        hidden,
        down,
        flops=2 * rows * hidden.shape[1] * width,
    )


def sort_rows(here, source_ref, out_refs, moves, array):
    for which, source, out, target, rows in moves:
        if which == array:
            first = pl.multiple_of(source(here), 16)
            out_refs[out][target(here) : target(here) + rows, :] = source_ref[pl.ds(first, rows), :]


def feed_forward_grads(place, hidden, grad_pre, normed, branch, moves, out_rows):
    half, width = normed[0].shape
    hidden_width = hidden[0].shape[1]

    def kernel(place_ref, *refs):
        hidden_refs, grad_refs = refs[0:2], refs[2:4]
        normed_refs, branch_refs = refs[4:8], refs[8:12]
        out_refs = refs[12:-2] if moves else refs[12:]
        up_ref, down_ref = refs[-2:] if moves else out_refs
        for target, lefts, rights in (
            (up_ref, normed_refs, grad_refs),
            (down_ref, hidden_refs, branch_refs),
        ):
            for begin in range(0, target.shape[0], 256):
                cut = slice(begin, begin + 256)
                total = 0.0
                for quarter in range(4):
                    rows = slice((quarter % 2) * half, (quarter % 2 + 1) * half)
                    if target is up_ref:
                        left, right = lefts[quarter][:, cut], rights[quarter // 2][rows, :]
                    else:
                        left, right = lefts[quarter // 2][rows, cut], rights[quarter][...]
                    total = total + contract_rows(left, right)
                target[cut, :] = total.astype(BF16)
        if moves:
            sort_rows(place_ref[4], up_ref, out_refs, moves, 0)
            sort_rows(place_ref[4], down_ref, out_refs, moves, 1)

    whole = [((width, hidden_width), BF16), ((hidden_width, width), BF16)]
    return local_call(
        kernel,
        [((rows, width), BF16) for rows in out_rows] if moves else whole,
        place,
        *hidden,
        *grad_pre,
        *normed,
        *branch,
        flops=16 * half * width * hidden_width,
        scratch=[pltpu.VMEM(shape, dtype) for shape, dtype in whole] if moves else [],
    )


def attention_grads(place, normed, grads, context, attended, sums, rank_sums, moves, out_rows):
    rows, width = normed[0].shape
    half = rows // 2
    rank_width = width // RANKS
    extra = sums.shape[0]
    columns = 3 * rank_width + extra
    column_moves, plane_moves = moves
    count = len(out_rows[0]) if column_moves else 1

    def kernel(place_ref, *refs):
        normed_refs, grad_refs, context_refs = refs[0:2], refs[2:4], refs[4:6]
        attended_refs, sums_ref, rank_ref = refs[6:10], refs[10], refs[11]
        outs = refs[12:-3] if column_moves else refs[12:-1]
        total_ref = refs[-1]
        rank = place_ref[1]
        target = refs[-3] if column_moves else outs[0]
        for begin in range(0, width, 256):
            cut = slice(begin, begin + 256)
            total = contract_rows(normed_refs[0][:, cut], grad_refs[0][...])
            total += contract_rows(normed_refs[1][:, cut], grad_refs[1][...])
            target[cut, 0 : 3 * rank_width] = total.astype(BF16)
        for other in range(RANKS):
            cut = slice(other * rank_width, (other + 1) * rank_width)
            total_ref[:, cut] = sums_ref[:, cut] + jnp.where(rank == other, rank_ref[...], 0.0)
        target[:, 3 * rank_width :] = total_ref[...].T.astype(BF16)
        total = 0.0
        for quarter in range(4):
            cut = slice((quarter % 2) * half, (quarter % 2 + 1) * half)
            total = total + contract_rows(
                context_refs[quarter // 2][cut, :], attended_refs[quarter][...]
            )
        plane_target = refs[-2] if column_moves else outs[1]
        plane_target[...] = total.astype(BF16)
        if column_moves:
            sort_rows(place_ref[4], target, outs[:count], column_moves, 0)
            sort_rows(place_ref[4], plane_target, outs[count:], plane_moves, 0)

    whole = [((width, columns), BF16), ((rank_width, width), BF16)]
    if column_moves:
        outs = [((rows_, columns), BF16) for rows_ in out_rows[0]]
        outs += [((rows_, width), BF16) for rows_ in out_rows[1]]
    else:
        outs = whole
    scratch = [pltpu.VMEM(shape, dtype) for shape, dtype in whole] if column_moves else []
    return local_call(
        kernel,
        outs,
        place,
        *normed,
        *grads,
        *context,
        *attended,
        sums,
        rank_sums,
        flops=4 * rows * width * columns + 4 * rows * rank_width * width,
        scratch=scratch + [pltpu.VMEM((extra, width), F32)],
    )


def norm_forward(place, inputs, shares, vectors):
    rows, width = inputs.shape

    def kernel(place_ref, inputs_ref, kept_ref, near_ref, far_ref, vectors_ref, mid_ref, normed_ref):
        for cut in row_chunks(rows):
            attended = kept_ref[cut, :] + near_ref[cut, :].astype(F32)
            attended += far_ref[cut, :].astype(F32)
            mid = inputs_ref[cut, :].astype(F32) + attended + vectors_ref[4:5, :]
            mid_ref[cut, :] = mid
            normed = normalize(mid)[0] * vectors_ref[5:6, :] + vectors_ref[6:7, :]
            normed_ref[cut, :] = normed.astype(BF16)

    return local_call(
        kernel, [((rows, width), F32), ((rows, width), BF16)], place, inputs, *shares, vectors
    )


def norm_grads(place, residual, values, shares, vectors, gain_row, with_sums):
    rows, width = residual.shape

    def kernel(
        place_ref, residual_ref, values_ref, kept_ref, near_ref, far_ref, vectors_ref, *out_refs
    ):
        totals = [jnp.zeros((1, width), F32)] * 3
        for cut in row_chunks(rows):
            grad = kept_ref[cut, :] + near_ref[cut, :].astype(F32)
            grad += far_ref[cut, :].astype(F32)
            normalized, inverse = normalize(values_ref[cut, :].astype(F32))
            gain = vectors_ref[gain_row : gain_row + 1, :]
            result = residual_ref[cut, :] + norm_backward(grad, normalized, inverse, gain)
            out_refs[0][cut, :] = result
            if with_sums:
                rounded = result.astype(BF16)
                out_refs[1][cut, :] = rounded
                terms = (grad * normalized, grad, rounded)
                totals = [total + column_sums(term) for total, term in zip(totals, terms)]
        if with_sums:
            for row, total in enumerate(totals):
                out_refs[2][row : row + 1, :] = total

    outs = [((rows, width), F32)]
    if with_sums:
        outs += [((rows, width), BF16), ((3, width), F32)]
    return local_call(kernel, outs, place, residual, values, *shares, vectors)


class Layout:
    def __init__(self, dp):
        self.dp = dp
        self.count = dp * 2
        self.planes = dp // 4
        self.direct = self.planes == 4
        self.dp_index = lax.axis_index("dp")
        self.core = lax.axis_index("seq")
        self.z = self.dp_index // 4
        self.y = (self.dp_index // 2) % 2
        self.x = self.dp_index % 2
        self.rank = (self.z % 2) * 2 + self.core

    def swap(self, values, mask):
        return swap(values, mask, self.count)

    def gather_tokens(self, values):
        across = self.swap(values, ALONG_Z)
        return (values, self.swap(values, CORE)), (across, self.swap(across, CORE))

    def scatter_tokens(self, own, far):
        crossing = (far[0] + self.swap(far[1], CORE).astype(F32)).astype(BF16)
        return own[0], self.swap(own[1], CORE), self.swap(crossing, ALONG_Z)

    def from_column(self, same, other):
        return (
            self.swap(other, ALONG_Z),
            self.swap(same, ALONG_Z2),
            self.swap(other, ALONG_Z | ALONG_Z2),
        )

    def spread_plane(self, first, second):
        first_x = self.swap(first, ALONG_X)
        second_y = self.swap(second, ALONG_Y)
        first_y = self.swap(jnp.concatenate([first, first_x]), ALONG_Y)
        second_x = self.swap(jnp.concatenate([second, second_y]), ALONG_X)
        return [first, first_x, first_y, second, second_y, second_x]

    def gather_columns(self, same, other):
        rows, columns = same.shape
        if not self.direct:
            return self.gather_columns_plainly(same, other)
        by_1, by_2, by_3 = self.from_column(same, other)
        spread = self.spread_plane(jnp.concatenate([same, by_2]), jnp.concatenate([by_1, by_3]))
        return move_blocks(
            spread, self.column_moves(rows, 2 * rows, 0), [self.dp * rows], self.dp_index
        )[0]

    def gather_columns_plainly(self, same, other):
        low = self.rank < 2
        both = jnp.stack([jnp.where(low, same, other), jnp.where(low, other, same)])
        whole = lax.all_gather(both, "dp", axis=0)
        mine = lax.dynamic_index_in_dim(whole, self.rank // 2, 1, keepdims=False)
        return mine.reshape(-1, same.shape[1])

    def column_moves(self, rows, stride, out):
        moves = []
        for far_z in range(2):
            first = far_z * rows
            for array, row, flip in (
                (0, first, 0),
                (1, first, 1),
                (2, first, 2),
                (2, stride + first, 3),
                (3, first, 4),
                (4, first, 6),
                (5, first, 5),
                (5, stride + first, 7),
            ):
                moves.append((array, always(row), out, xor_row(flip + 8 * far_z, rows), rows))
        return moves

    def gather_plane_rows(self, shard):
        rows, columns = shard.shape
        if not self.direct:
            whole = lax.all_gather(shard, "dp", axis=0, tiled=True)
            quarter = self.dp * rows // RANKS
            return lax.dynamic_slice_in_dim(whole, self.rank * quarter, quarter, 0)
        mine = lax.ppermute(shard, AXES, plane_route(self.planes))
        by_x = self.swap(mine, ALONG_X)
        by_y = self.swap(jnp.concatenate([mine, by_x]), ALONG_Y)
        sources = ((0, 0, 0), (1, 0, 1), (2, 0, 2), (2, rows, 3))
        moves = [
            (array, always(row), 0, xor_row(flip, rows, 0, 3), rows) for array, row, flip in sources
        ]
        return move_blocks([mine, by_x, by_y], moves, [4 * rows], self.dp_index)[0]

    def feed_forward_blocks(self, w_up, w_down):
        shard, hidden = w_up.shape
        columns = hidden // RANKS
        same = lax.dynamic_slice_in_dim(w_up, self.rank * columns, columns, 1)
        other = lax.dynamic_slice_in_dim(w_up, (self.rank ^ 2) * columns, columns, 1)
        if not self.direct:
            return same, other
        by_1, by_2, by_3 = self.from_column(same, other)
        mine = lax.ppermute(w_down, AXES, plane_route(self.planes))
        half = w_down.shape[0] // 2
        return (
            jnp.concatenate([same, by_2, mine[:half]]),
            jnp.concatenate([by_1, by_3, mine[half:]]),
        )

    def place_feed_forward(self, arrays, shard, rows):
        half = rows // 2
        moves = []
        for flip in range(4):
            for odd in range(2):
                array = 4 * odd + flip
                for far_z in range(2):
                    target = xor_row(flip + 4 * (odd + 2 * far_z), shard)
                    moves.append((array, always(far_z * shard), 0, target, shard))
                target = xor_row(flip, rows, odd * half, 3)
                moves.append((array, always(2 * shard), 1, target, half))
        return move_blocks(arrays, moves, [self.dp * shard, 4 * rows], self.dp_index)

    def sum_first(self, kept, received):
        both = kept.astype(F32) + received.astype(F32)
        rows = both.shape[0] // 2
        return both[:rows], both[rows:].astype(BF16)

    def across_column(self, first, second, rows):
        blocks = jnp.stack([first[:rows], second[:rows], first[rows : 2 * rows], second[rows : 2 * rows]])
        blocks = blocks.reshape(4, 2, rows // 2, first.shape[1])
        mine = lax.dynamic_index_in_dim(blocks, self.core, 1, keepdims=False)
        away = lax.dynamic_index_in_dim(blocks, 1 - self.core, 1, keepdims=False).astype(BF16)
        both = jnp.stack([mine.astype(BF16), self.swap(away, CORE)], axis=1)
        return both[0], [self.swap(both[step], step * ALONG_Z) for step in range(1, 4)]

    def sum_column(self, both, by):
        near = both.astype(F32) + by[1].astype(F32)
        far = by[0].astype(F32) + by[2].astype(F32)
        return self.in_rank_order([near[0], near[1], far[0], far[1]])

    def in_rank_order(self, ranks):
        high, low = self.rank // 2 == 1, self.rank % 2 == 1
        ranks = [jnp.where(low, ranks[i ^ 1], ranks[i]) for i in range(4)]
        return [jnp.where(high, ranks[i ^ 2], ranks[i]) for i in range(4)]

    def column_parts(self, rows, extra, array):
        moves = []
        half = 2 * rows + extra
        for out, flips in enumerate(((0, 1), (2, 3), (4, 6), (5, 7))):
            for block, flip in enumerate(flips):
                for far_z in range(2):
                    target = block * half + far_z * rows
                    moves.append(
                        (array, xor_row(flip + 8 * far_z, rows), out, always(target), rows)
                    )
        return moves

    def column_order(self, rows):
        return (self.column_parts(rows, 0, 0), [4 * rows] * 4) if self.direct else ([], [])

    def scatter_columns_plainly(self, grads):
        dp, rows, columns = self.dp, grads.shape[0] // self.dp, grads.shape[1]
        whole = jnp.zeros((dp * rows, RANKS, columns), BF16)
        whole = lax.dynamic_update_slice_in_dim(whole, grads[:, None, :], self.rank, 1)
        mine = lax.psum_scatter(
            whole.reshape(dp * rows, RANKS * columns).astype(F32),
            AXES,
            scatter_dimension=0,
            tiled=True,
        )
        return [mine[:, rank * columns : (rank + 1) * columns] for rank in range(RANKS)]

    def plane_order(self, rows):
        if not self.direct:
            return [], []
        moves = [
            (0, xor_row(flip, rows, 0, 3), flip // 2, always(flip % 2 * rows), rows)
            for flip in range(4)
        ]
        return moves, [2 * rows] * 2

    def scatter_plane_rows_plainly(self, grads):
        rows, columns = grads.shape
        whole = jnp.zeros((RANKS, rows, columns), BF16)
        whole = lax.dynamic_update_slice_in_dim(whole, grads[None], self.rank, 0)
        return lax.psum_scatter(
            whole.reshape(RANKS * rows, columns).astype(F32),
            AXES,
            scatter_dimension=0,
            tiled=True,
        )

    def to_owners(self, lower, upper):
        back = [(target, source) for source, target in plane_route(self.planes)]
        crossed = [(source, target ^ CORE) for source, target in back]
        high = self.z // 2 == 1
        straight = jnp.where(high, upper, lower).astype(BF16)
        other = jnp.where(high, lower, upper).astype(BF16)
        return lax.ppermute(straight, AXES, back), lax.ppermute(other, AXES, crossed)

    def feed_forward_order(self, shard, rows):
        if not self.direct:
            return [], []
        half = rows // 2
        stride = 2 * shard + half
        moves = self.column_parts(shard, half, 0)
        for out, (flips, upper) in enumerate((((0, 1), 0), ((2, 3), 0), ((0, 2), 1), ((1, 3), 1))):
            for block, flip in enumerate(flips):
                target = always(block * stride + 2 * shard)
                moves.append((1, xor_row(flip, rows, upper * half, 3), out, target, half))
        return moves, [2 * stride] * 4


def on_device(
    dp,
    inputs,
    lengths,
    cotangent,
    norm1_gain,
    norm1_shift,
    w_query,
    b_query,
    w_key,
    w_value,
    b_value,
    w_output,
    b_output,
    norm2_gain,
    norm2_shift,
    w_up,
    b_up,
    w_down,
    b_down,
):
    at = Layout(dp)
    tokens, width = inputs.shape
    shard = w_query.shape[0]
    hidden_width = w_up.shape[1]
    rank_width = width // RANKS
    rank_hidden = hidden_width // RANKS

    partner_length = at.swap(lengths, ALONG_Z)
    place = jnp.stack([at.core, at.rank, lengths[0], partner_length[0], at.dp_index])
    place = place.astype(jnp.int32)
    here = jnp.stack([at.core, at.rank]).astype(jnp.int32)

    vectors = [norm1_gain, norm1_shift, b_query, b_value, b_output, norm2_gain, norm2_shift, b_down]
    extra = len(vectors) + b_up.shape[0] // shard
    same, other = cut_projections(here, (w_query, w_key, w_value), (*vectors, b_up))
    own_inputs, far_inputs = at.gather_tokens(inputs)
    qkv = at.gather_columns(same, other)
    vectors = qkv[:, 3 * rank_width :].astype(F32).T
    up_bias = vectors[8:].reshape(extra - 8, dp, shard).transpose(1, 0, 2).reshape(1, hidden_width)
    up_bias = lax.dynamic_slice_in_dim(up_bias, at.rank * rank_hidden, rank_hidden, 1)
    out_rows = at.gather_plane_rows(w_output)

    positions = at.core * tokens + jnp.arange(tokens, dtype=jnp.int32)
    own_valid = (positions < lengths[0]).astype(F32)[:, None]
    grad_out = cotangent.astype(F32) * own_valid
    grad_branch = grad_out.astype(BF16)
    branch_across = at.swap(grad_branch, ALONG_Z)
    first, second = at.feed_forward_blocks(w_up, w_down)
    to_x = lambda values: at.swap(values, ALONG_X)
    to_y = lambda values: at.swap(values, ALONG_Y)

    far_clip = attention_forward(place, 1, far_inputs, qkv, vectors, out_rows)
    if at.direct:
        far_clip, first_x, second_y, branch_across = together(
            far_clip, to_x(first), to_y(second), branch_across
        )
    crossing = (far_clip[3] + at.swap(far_clip[4], CORE).astype(F32)).astype(BF16)
    far_share = at.swap(crossing, ALONG_Z)
    own_clip = attention_forward(place, 0, tie(own_inputs, crossing), qkv, vectors, out_rows)
    near_share = at.swap(own_clip[4], CORE)
    if at.direct:
        own_clip, far_share, first_y, second_x = together(
            own_clip, far_share, to_y(first), to_x(second)
        )
    mid, normed2 = norm_forward(place, inputs, (own_clip[3], near_share, far_share), vectors)

    far_normed2 = at.swap(normed2, ALONG_Z)
    own_normed2 = (normed2, at.swap(normed2, CORE))
    if at.direct:
        far_normed2, first_xy, second_yx = together(far_normed2, to_y(first_x), to_x(second_y))
        arrays = [first, first_x, first_y, first_xy, second, second_x, second_y, second_yx]
        up, down = at.place_feed_forward(arrays, shard, w_down.shape[0])
    else:
        up, down = at.gather_columns_plainly(first, second), at.gather_plane_rows(w_down)
    early = tie(grad_branch, mid)
    own_branch = (grad_branch, at.swap(early, CORE))
    branch_across = tie(branch_across, mid)
    far_branch = (branch_across, at.swap(branch_across, CORE))
    far_normed2 = (far_normed2, at.swap(far_normed2, CORE))

    own = feed_forward(place, own_normed2, own_branch, up, down, up_bias)
    far = feed_forward(place, far_normed2, far_branch, up, down, up_bias)
    shares = at.scatter_tokens(own[3:], far[3:])
    grad_mid, grad_attended, norm2_sums = norm_grads(
        place, grad_out, mid, shares, vectors, 5, True
    )
    moves, sizes = at.feed_forward_order(shard, hidden_width // dp)
    sorted_grads = feed_forward_grads(
        place,
        (own[0], far[0]),
        (own[1], far[1]),
        own_normed2 + far_normed2,
        own_branch + far_branch,
        moves,
        sizes,
    )
    own_out, far_out = feed_forward_out(place, tie(own[0], far[4]), down), feed_forward_out(place, far[0], down)
    out_near = at.swap(own_out[1], CORE)
    out_crossing = (far_out[0] + at.swap(far_out[1], CORE).astype(F32)).astype(BF16)

    across = at.swap(grad_attended, ALONG_Z)
    own_attended = (grad_attended, at.swap(grad_attended, CORE))
    own_back = attention_backward(
        place, 0, own_attended, own_inputs, own_clip[1], qkv, vectors, out_rows
    )
    across = tie(across, own_back[2])
    far_attended = (across, at.swap(across, CORE))
    out_far = at.swap(tie(out_crossing, across), ALONG_Z)
    far_back = attention_backward(
        place, 1, far_attended, far_inputs, far_clip[1], qkv, vectors, out_rows
    )

    if at.direct:
        kept_1, sent_1, kept_2, sent_2 = sorted_grads
        up_first = at.sum_first(tie(kept_1, own_back[2]), at.swap(sent_1, ALONG_Y))
        up_second = at.sum_first(tie(kept_2, own_back[2]), at.swap(sent_2, ALONG_X))
        up_received = at.swap(up_first[1], ALONG_X), at.swap(up_second[1], ALONG_Y)
    else:
        grad_w_up = at.scatter_columns_plainly(sorted_grads[0])
        grad_w_down = at.scatter_plane_rows_plainly(sorted_grads[1])

    norm1_sums = own_back[3] + far_back[3]
    head_sums = own_back[4] + far_back[4]
    up_sums = (own[2] + far[2]).reshape(2 * dp // RANKS, extra - 8, shard // 2)
    up_sums = up_sums.transpose(1, 0, 2).reshape(extra - 8, rank_width)
    branch_sums = column_sums(grad_branch)
    nothing = jnp.zeros((2, width), F32)
    sums = jnp.concatenate(
        [norm1_sums, nothing, norm2_sums[2:], norm2_sums[:2], branch_sums, nothing, nothing]
    )
    nothing = jnp.zeros((4, rank_width), F32)
    rank_sums = jnp.concatenate(
        [
            nothing[:2],
            head_sums[:, :rank_width],
            head_sums[:, 2 * rank_width :],
            nothing,
            up_sums,
        ]
    )
    column_moves, column_sizes = at.column_order(shard)
    plane_moves, plane_sizes = at.plane_order(shard)
    sorted_grads = attention_grads(
        place,
        (own_clip[0], far_clip[0]),
        (own_back[0], far_back[0]),
        (own_clip[2], far_clip[2]),
        own_attended + far_attended,
        sums,
        rank_sums,
        (column_moves, plane_moves),
        (column_sizes, plane_sizes),
    )
    back_near = at.swap(own_back[2], CORE)
    back_crossing = (far_back[1] + at.swap(far_back[2], CORE).astype(F32)).astype(BF16)
    if at.direct:
        half = shard // 2
        *sorted_grads, out_far, back_far, received_1, received_2 = together(
            *sorted_grads, out_far, at.swap(back_crossing, ALONG_Z), *up_received
        )
        kept_1, sent_1, kept_2, sent_2, output_kept, output_sent = sorted_grads
        first, second = up_first[0] + received_1.astype(F32), up_second[0] + received_2.astype(F32)
        up_both, up_by = at.across_column(first, second, shard)
        received_1, received_2, output_sent, *up_by = together(
            at.swap(sent_1, ALONG_Y), at.swap(sent_2, ALONG_X), output_sent, *up_by
        )
        qkv_first, qkv_second = at.sum_first(kept_1, received_1), at.sum_first(kept_2, received_2)
        received_1, received_2, output_sent, *owners = together(
            at.swap(qkv_first[1], ALONG_X),
            at.swap(qkv_second[1], ALONG_Y),
            at.swap(output_sent, ALONG_Y),
            *at.to_owners(first[2 * shard :], second[2 * shard :]),
        )
        grad_w_down = owners[0].astype(F32) + owners[1].astype(F32)
        grad_w_up = at.sum_column(up_both, up_by)
        first = qkv_first[0] + received_1.astype(F32)
        second = qkv_second[0] + received_2.astype(F32)
        output_first = at.sum_first(output_kept, output_sent)
        grad_output = output_first[0] + at.swap(output_first[1], ALONG_X).astype(F32)
        both, by = at.across_column(first, second, shard)
        *by, lower, upper = together(*by, *at.to_owners(grad_output[:half], grad_output[half:]))
        by_rank = at.sum_column(both, by)
        grad_w_output = lower.astype(F32) + upper.astype(F32)
    else:
        back_far = at.swap(back_crossing, ALONG_Z)
        by_rank = at.scatter_columns_plainly(sorted_grads[0])
        grad_w_output = at.scatter_plane_rows_plainly(sorted_grads[1])
    shares = (own_back[1], back_near, back_far)
    (input_grad,) = norm_grads(place, grad_mid, inputs, shares, vectors, 0, False)
    grad_w_up = jnp.concatenate(grad_w_up, axis=1)
    branch = own_out[0] + out_near.astype(F32) + out_far.astype(F32)
    output = (mid + branch + vectors[7:8]).astype(BF16)
    grad_w_query, grad_w_key, grad_w_value = (
        jnp.concatenate([part[:, i * rank_width : (i + 1) * rank_width] for part in by_rank], axis=1)
        for i in range(3)
    )
    sums = sum(part[:, 3 * rank_width :] for part in by_rank)
    shares = [sums[:, i] for i in range(8)] + [sums[:, 8:].T.reshape(-1)]
    return (
        output,
        input_grad,
        shares[0],
        shares[1],
        grad_w_query,
        shares[2],
        grad_w_key,
        grad_w_value,
        shares[3],
        grad_w_output,
        shares[4],
        shares[5],
        shares[6],
        grad_w_up,
        shares[8],
        grad_w_down,
        shares[7],
    )


def solution(mesh):
    rows, vector = P("dp", None), P("dp")
    own_rows, own_vector = P(AXES, None), P(AXES)
    return jax.shard_map(
        functools.partial(on_device, mesh.shape["dp"]),
        mesh=mesh,
        in_specs=(
            own_rows,
            vector,
            own_rows,
            vector,
            vector,
            rows,
            vector,
            rows,
            rows,
            vector,
            rows,
            vector,
            vector,
            vector,
            rows,
            vector,
            rows,
            vector,
        ),
        out_specs=(
            own_rows,
            own_rows,
            own_vector,
            own_vector,
            own_rows,
            own_vector,
            own_rows,
            own_rows,
            own_vector,
            own_rows,
            own_vector,
            own_vector,
            own_vector,
            own_rows,
            own_vector,
            own_rows,
            own_vector,
        ),
        check_vma=False,
    )
```

```python
import functools
import math

import jax
import jax.numpy as jnp
from jax import lax
from jax.experimental import pallas as pl
from jax.experimental.pallas import tpu as pltpu
from jax.sharding import PartitionSpec as P

HEAD = 80
EPS_NORM = 1e-05
MASKED = -1e30
RANKS = 4
AXES = ("dp", "seq")
BF16 = jnp.bfloat16
F32 = jnp.float32

CORE, ALONG_X, ALONG_Y, ALONG_Z, ALONG_Z2 = 1, 2, 4, 8, 16


def swap(values, mask, count):
    return lax.ppermute(values, AXES, [(place, place ^ mask) for place in range(count)])


def plane_route(planes):
    pairs = []
    for column in range(4):
        for plane in range(planes):
            for core in range(2):
                target_z = (plane >> 1) + 2 * core
                pairs.append(
                    (
                        (plane * 4 + column) * 2 + core,
                        (target_z * 4 + column) * 2 + (plane & 1),
                    )
                )
    return pairs


def move_blocks(arrays, moves, out_rows, place, extra=0):
    columns = arrays[0].shape[1]
    shapes = [jax.ShapeDtypeStruct((rows, columns), arrays[0].dtype) for rows in out_rows]
    if extra:
        shapes.append(jax.ShapeDtypeStruct((extra, out_rows[0]), F32))

    def kernel(place_ref, *refs):
        in_refs, out_refs, sems = refs[: len(arrays)], refs[len(arrays) : -1], refs[-1]
        here = place_ref[0]
        copies = []
        for index, (array, source, out, target, rows) in enumerate(moves):
            source = pl.multiple_of(source(here), 8)
            target = pl.multiple_of(target(here), 8)
            copy = pltpu.make_async_copy(
                in_refs[array].at[pl.ds(source, rows)],
                out_refs[out].at[pl.ds(target, rows)],
                sems.at[index],
            )
            copy.start()
            copies.append(copy)
        for copy in copies:
            copy.wait()
        if extra:
            out_refs[-1][...] = out_refs[0][:, columns - extra :].astype(F32).T

    return pl.pallas_call(
        kernel,
        out_shape=shapes,
        in_specs=[pl.BlockSpec(memory_space=pltpu.SMEM)]
        + [pl.BlockSpec(memory_space=pl.ANY)] * len(arrays),
        out_specs=[pl.BlockSpec(memory_space=pltpu.VMEM)] * len(shapes),
        scratch_shapes=[pltpu.SemaphoreType.DMA((len(moves),))],
        compiler_params=pltpu.CompilerParams(vmem_limit_bytes=32 * 1024 * 1024),
    )(jnp.reshape(place, (1,)).astype(jnp.int32), *arrays)


def always(row):
    return lambda here: row


def xor_row(flip, rows, first=0, mask=15):
    return lambda here: jnp.bitwise_xor(jnp.bitwise_and(here, mask), flip) * rows + first


def tie(values, *others):
    return lax.optimization_barrier((values,) + others)[0]


def together(*values):
    return lax.optimization_barrier(values)


def rows_times(operand, weight):
    return lax.dot_general(operand, weight, (((1,), (0,)), ((), ())), preferred_element_type=F32)


def times_transposed(operand, weight):
    return lax.dot_general(operand, weight, (((1,), (1,)), ((), ())), preferred_element_type=F32)


def contract_rows(operand, other):
    return lax.dot_general(operand, other, (((0,), (0,)), ((), ())), preferred_element_type=F32)


def normalize(values):
    average = jnp.mean(values, axis=-1, keepdims=True)
    centred = values - average
    inverse = lax.rsqrt(jnp.mean(centred * centred, axis=-1, keepdims=True) + EPS_NORM)
    return (centred * inverse, inverse)


def norm_backward(grad_normed, normalized, inverse, norm_gain):
    scaled = grad_normed * norm_gain
    return inverse * (
        scaled
        - jnp.mean(scaled, axis=-1, keepdims=True)
        - normalized * jnp.mean(scaled * normalized, axis=-1, keepdims=True)
    )


def column_sums(values):
    return jnp.sum(values.astype(F32), axis=0, keepdims=True)


def local_call(kernel, outs, *operands, flops=0, scratch=(), limit=32):
    vmem = pl.BlockSpec(memory_space=pltpu.VMEM)
    shapes = [jax.ShapeDtypeStruct(shape, dtype) for shape, dtype in outs]
    moved = sum(math.prod(shape) * jnp.dtype(dtype).itemsize for shape, dtype in outs)
    moved += sum(operand.size * operand.dtype.itemsize for operand in operands)
    return pl.pallas_call(
        kernel,
        out_shape=shapes,
        in_specs=[pl.BlockSpec(memory_space=pltpu.SMEM)] + [vmem] * (len(operands) - 1),
        out_specs=[vmem] * len(outs),
        scratch_shapes=list(scratch),
        compiler_params=pltpu.CompilerParams(vmem_limit_bytes=limit * 1024 * 1024),
        cost_estimate=pl.CostEstimate(flops=flops * 20, bytes_accessed=moved * 20, transcendentals=0),
    )(*operands)


CHUNK = 64


def row_chunks(rows):
    return [slice(first, min(first + CHUNK, rows)) for first in range(0, rows, CHUNK)]


def head_slice(part, head, heads):
    first = (part * heads + head) * HEAD
    return slice(first, first + HEAD)


def cut_projections(place, projections, vectors):
    shard, width = projections[0].shape
    rank_width = width // RANKS
    extra = sum(vector.shape[0] for vector in vectors) // shard
    columns = 3 * rank_width + extra

    operands = (*projections, *vectors)

    def kernel(place_ref, *refs):
        sources, refs = refs[: len(operands)], refs[len(operands) :]
        same_ref, other_ref, blocks, rows = refs[:4]
        held, sems = refs[4:-1], refs[-1]
        copies = [
            pltpu.make_async_copy(source, target, sems.at[index])
            for index, (source, target) in enumerate(zip(sources, held))
        ]
        for copy in copies:
            copy.start()
        for copy in copies:
            copy.wait()
        projection_refs, vector_refs = held[:3], held[3:]
        row = 0
        for ref in vector_refs:
            values = ref[...].astype(F32)
            for first in range(0, ref.shape[0], shard):
                rows[row : row + 1, :] = values[first : first + shard].reshape(1, shard)
                row += 1
        turned = rows[...].T.astype(BF16)
        for rank in range(RANKS):
            cut = slice(rank * rank_width, (rank + 1) * rank_width)
            for part, ref in enumerate(projection_refs):
                blocks[rank, :, part * rank_width : (part + 1) * rank_width] = ref[:, cut]
            blocks[rank, :, 3 * rank_width :] = turned
        other_ref[...] = blocks[jnp.bitwise_xor(place_ref[1], 2)]
        same_ref[...] = blocks[place_ref[1]]

    return pl.pallas_call(
        kernel,
        out_shape=[jax.ShapeDtypeStruct((shard, columns), BF16)] * 2,
        in_specs=[pl.BlockSpec(memory_space=pltpu.SMEM)]
        + [pl.BlockSpec(memory_space=pl.ANY)] * len(operands),
        out_specs=[pl.BlockSpec(memory_space=pltpu.VMEM)] * 2,
        scratch_shapes=[
            pltpu.VMEM((RANKS, shard, columns), BF16),
            pltpu.VMEM((extra, shard), F32),
            *(pltpu.VMEM(operand.shape, operand.dtype) for operand in operands),
            pltpu.SemaphoreType.DMA((len(operands),)),
        ],
        compiler_params=pltpu.CompilerParams(vmem_limit_bytes=56 * 1024 * 1024),
    )(place, *operands)


def attention_forward(place, clip, inputs, qkv, vectors, out_rows):
    half, width = inputs[0].shape
    rows = 2 * half
    rank_width = width // RANKS
    heads = rank_width // HEAD
    scale = 1.0 / math.sqrt(HEAD)

    def kernel(
        place_ref,
        first_ref,
        second_ref,
        qkv_ref,
        vectors_ref,
        out_rows_ref,
        normed_ref,
        projected_ref,
        context_ref,
        kept_ref,
        sent_ref,
    ):
        core, rank, length = place_ref[0], place_ref[1], place_ref[2 + clip]
        gain, shift = vectors_ref[0:1, :], vectors_ref[1:2, :]
        for index, ref in enumerate((first_ref, second_ref)):
            for cut in row_chunks(half):
                normed = normalize(ref[cut, :].astype(F32))[0] * gain + shift
                normed_ref[index * half + cut.start : index * half + cut.stop, :] = normed.astype(
                    BF16
                )
        bias = jnp.zeros((1, rank_width), F32)
        value_bias = bias
        for other in range(RANKS):
            cut = slice(other * rank_width, (other + 1) * rank_width)
            bias += jnp.where(rank == other, vectors_ref[2:3, cut], 0.0)
            value_bias += jnp.where(rank == other, vectors_ref[3:4, cut], 0.0)
        biases = (bias, None, value_bias)
        projected = rows_times(normed_ref[...], qkv_ref[...])
        for part, added in enumerate(biases):
            values = projected[:, part * rank_width : (part + 1) * rank_width]
            values = values if added is None else values + added
            projected_ref[:, part * rank_width : (part + 1) * rank_width] = values.astype(BF16)
        positions = lax.broadcasted_iota(jnp.int32, (rows, rows), 1)
        positions = jnp.bitwise_and(positions + core * half, rows - 1)
        valid = positions < length
        for head in range(heads):
            queries = projected_ref[:, head_slice(0, head, heads)]
            keys = projected_ref[:, head_slice(1, head, heads)]
            values = projected_ref[:, head_slice(2, head, heads)]
            scores = jnp.where(valid, times_transposed(queries, keys) * scale, MASKED)
            weights = jnp.exp(scores - jnp.max(scores, axis=1, keepdims=True))
            weights = weights * (1.0 / jnp.sum(weights, axis=1, keepdims=True))
            context = rows_times(weights.astype(BF16), values)
            context_ref[:, head_slice(0, head, heads)] = context.astype(BF16)
        kept_ref[...] = rows_times(context_ref[0:half, :], out_rows_ref[...])
        sent_ref[...] = rows_times(context_ref[half:rows, :], out_rows_ref[...]).astype(BF16)

    return local_call(
        kernel,
        [
            ((rows, width), BF16),
            ((rows, 3 * rank_width), BF16),
            ((rows, rank_width), BF16),
            ((half, width), F32),
            ((half, width), BF16),
        ],
        place,
        *inputs,
        qkv,
        vectors,
        out_rows,
        flops=2 * rows * width * width + 4 * rows * rows * rank_width,
    )


def attention_backward(place, clip, grads, inputs, projected, qkv, vectors, out_rows):
    half, width = inputs[0].shape
    rows = 2 * half
    rank_width = width // RANKS
    heads = rank_width // HEAD
    scale = 1.0 / math.sqrt(HEAD)

    def kernel(
        place_ref,
        grad_first_ref,
        grad_second_ref,
        first_ref,
        second_ref,
        projected_ref,
        qkv_ref,
        vectors_ref,
        out_rows_ref,
        grads_ref,
        kept_ref,
        sent_ref,
        norm_sums_ref,
        head_sums_ref,
        context_ref,
        normed_ref,
    ):
        core, length = place_ref[0], place_ref[2 + clip]
        for index, ref in enumerate((grad_first_ref, grad_second_ref)):
            context_ref[index * half : (index + 1) * half, :] = times_transposed(
                ref[...], out_rows_ref[...]
            ).astype(BF16)
        positions = lax.broadcasted_iota(jnp.int32, (rows, rows), 0)
        positions = jnp.bitwise_and(positions + core * half, rows - 1)
        valid = positions < length
        for head in range(heads):
            queries = projected_ref[:, head_slice(0, head, heads)]
            keys = projected_ref[:, head_slice(1, head, heads)]
            values = projected_ref[:, head_slice(2, head, heads)]
            grad_context = context_ref[:, head_slice(0, head, heads)]
            scores = jnp.where(valid, times_transposed(keys, queries) * scale, MASKED)
            weights = jnp.exp(scores - jnp.max(scores, axis=0, keepdims=True))
            weights = weights * (1.0 / jnp.sum(weights, axis=0, keepdims=True))
            grad_weights = times_transposed(values, grad_context)
            inner = jnp.sum(weights * grad_weights, axis=0, keepdims=True)
            grad_scores = (weights * (grad_weights - inner)).astype(BF16)
            grad_query = contract_rows(grad_scores, keys) * scale
            grad_key = rows_times(grad_scores, queries) * scale
            grad_value = rows_times(weights.astype(BF16), grad_context)
            grads_ref[:, head_slice(0, head, heads)] = grad_query.astype(BF16)
            grads_ref[:, head_slice(1, head, heads)] = grad_key.astype(BF16)
            grads_ref[:, head_slice(2, head, heads)] = grad_value.astype(BF16)
        head_sums_ref[...] = column_sums(grads_ref[...])
        weight = qkv_ref[:, 0 : 3 * rank_width]
        gain_sum = jnp.zeros((1, width), F32)
        shift_sum = jnp.zeros((1, width), F32)
        for index, ref in enumerate((first_ref, second_ref)):
            normed_ref[...] = times_transposed(
                grads_ref[index * half : (index + 1) * half, :], weight
            )
            for cut in row_chunks(half):
                grad = normed_ref[cut, :]
                if index == 0:
                    kept_ref[cut, :] = grad
                else:
                    sent_ref[cut, :] = grad.astype(BF16)
                gain_sum += column_sums(grad * normalize(ref[cut, :].astype(F32))[0])
                shift_sum += column_sums(grad)
        norm_sums_ref[0:1, :] = gain_sum
        norm_sums_ref[1:2, :] = shift_sum

    return local_call(
        kernel,
        [
            ((rows, 3 * rank_width), BF16),
            ((half, width), F32),
            ((half, width), BF16),
            ((2, width), F32),
            ((1, 3 * rank_width), F32),
        ],
        place,
        *grads,
        *inputs,
        projected,
        qkv,
        vectors,
        out_rows,
        flops=2 * rows * width * width + 10 * rows * rows * rank_width,
        scratch=[pltpu.VMEM((rows, rank_width), BF16), pltpu.VMEM((half, width), F32)],
    )


def feed_forward(place, normed, branch, up, down, up_bias):
    half, width = normed[0].shape
    rows = 2 * half
    hidden_width = up.shape[1]
    chunk = 256

    def kernel(
        place_ref,
        first_ref,
        second_ref,
        branch_first_ref,
        branch_second_ref,
        up_ref,
        down_ref,
        bias_ref,
        hidden_ref,
        grad_ref,
        sums_ref,
        kept_ref,
        sent_ref,
    ):
        for begin in range(0, hidden_width, chunk):
            cut = slice(begin, begin + chunk)
            total = jnp.zeros((1, chunk), F32)
            for index, (ref, branch_ref) in enumerate(
                ((first_ref, branch_first_ref), (second_ref, branch_second_ref))
            ):
                here = slice(index * half, (index + 1) * half)
                pre = rows_times(ref[...], up_ref[:, cut]) + bias_ref[:, cut]
                grad_hidden = times_transposed(branch_ref[...], down_ref[cut, :])
                share = 0.5 * (1.0 + lax.erf(pre * math.sqrt(0.5)))
                hidden_ref[here, cut] = (pre * share).astype(BF16)
                slope = share + pre * (jnp.exp(-0.5 * pre * pre) * (1.0 / math.sqrt(2.0 * math.pi)))
                grad = (grad_hidden * slope).astype(BF16)
                grad_ref[here, cut] = grad
                total += column_sums(grad)
            sums_ref[:, cut] = total
        kept_ref[...] = times_transposed(grad_ref[0:half, :], up_ref[...])
        sent_ref[...] = times_transposed(grad_ref[half:rows, :], up_ref[...]).astype(BF16)

    return local_call(
        kernel,
        [
            ((rows, hidden_width), BF16),
            ((rows, hidden_width), BF16),
            ((1, hidden_width), F32),
            ((half, width), F32),
            ((half, width), BF16),
        ],
        place,
        *normed,
        *branch,
        up,
        down,
        up_bias,
        flops=6 * rows * width * hidden_width,
    )


def feed_forward_out(place, hidden, down):
    rows, width = hidden.shape[0], down.shape[1]
    half = rows // 2

    def kernel(place_ref, hidden_ref, down_ref, kept_ref, sent_ref):
        kept_ref[...] = rows_times(hidden_ref[0:half, :], down_ref[...])
        sent_ref[...] = rows_times(hidden_ref[half:rows, :], down_ref[...]).astype(BF16)

    return local_call(
        kernel,
        [((half, width), F32), ((half, width), BF16)],
        place,
        hidden,
        down,
        flops=2 * rows * hidden.shape[1] * width,
    )


def sort_rows(here, source_ref, out_refs, moves, array):
    for which, source, out, target, rows in moves:
        if which == array:
            first = pl.multiple_of(source(here), 16)
            out_refs[out][target(here) : target(here) + rows, :] = source_ref[pl.ds(first, rows), :]


def feed_forward_grads(place, hidden, grad_pre, normed, branch, moves, out_rows):
    half, width = normed[0].shape
    hidden_width = hidden[0].shape[1]

    def kernel(place_ref, *refs):
        hidden_refs, grad_refs = refs[0:2], refs[2:4]
        normed_refs, branch_refs = refs[4:8], refs[8:12]
        out_refs = refs[12:-2] if moves else refs[12:]
        up_ref, down_ref = refs[-2:] if moves else out_refs
        for target, lefts, rights in (
            (up_ref, normed_refs, grad_refs),
            (down_ref, hidden_refs, branch_refs),
        ):
            for begin in range(0, target.shape[0], 256):
                cut = slice(begin, begin + 256)
                total = 0.0
                for quarter in range(4):
                    rows = slice((quarter % 2) * half, (quarter % 2 + 1) * half)
                    if target is up_ref:
                        left, right = lefts[quarter][:, cut], rights[quarter // 2][rows, :]
                    else:
                        left, right = lefts[quarter // 2][rows, cut], rights[quarter][...]
                    total = total + contract_rows(left, right)
                target[cut, :] = total.astype(BF16)
        if moves:
            sort_rows(place_ref[4], up_ref, out_refs, moves, 0)
            sort_rows(place_ref[4], down_ref, out_refs, moves, 1)

    whole = [((width, hidden_width), BF16), ((hidden_width, width), BF16)]
    return local_call(
        kernel,
        [((rows, width), BF16) for rows in out_rows] if moves else whole,
        place,
        *hidden,
        *grad_pre,
        *normed,
        *branch,
        flops=16 * half * width * hidden_width,
        scratch=[pltpu.VMEM(shape, dtype) for shape, dtype in whole] if moves else [],
    )


def attention_grads(place, normed, grads, context, attended, sums, rank_sums, moves, out_rows):
    rows, width = normed[0].shape
    half = rows // 2
    rank_width = width // RANKS
    extra = sums.shape[0]
    columns = 3 * rank_width + extra
    column_moves, plane_moves = moves
    count = len(out_rows[0]) if column_moves else 1

    def kernel(place_ref, *refs):
        normed_refs, grad_refs, context_refs = refs[0:2], refs[2:4], refs[4:6]
        attended_refs, sums_ref, rank_ref = refs[6:10], refs[10], refs[11]
        outs = refs[12:-3] if column_moves else refs[12:-1]
        total_ref = refs[-1]
        rank = place_ref[1]
        target = refs[-3] if column_moves else outs[0]
        for begin in range(0, width, 256):
            cut = slice(begin, begin + 256)
            total = contract_rows(normed_refs[0][:, cut], grad_refs[0][...])
            total += contract_rows(normed_refs[1][:, cut], grad_refs[1][...])
            target[cut, 0 : 3 * rank_width] = total.astype(BF16)
        for other in range(RANKS):
            cut = slice(other * rank_width, (other + 1) * rank_width)
            total_ref[:, cut] = sums_ref[:, cut] + jnp.where(rank == other, rank_ref[...], 0.0)
        target[:, 3 * rank_width :] = total_ref[...].T.astype(BF16)
        total = 0.0
        for quarter in range(4):
            cut = slice((quarter % 2) * half, (quarter % 2 + 1) * half)
            total = total + contract_rows(
                context_refs[quarter // 2][cut, :], attended_refs[quarter][...]
            )
        plane_target = refs[-2] if column_moves else outs[1]
        plane_target[...] = total.astype(BF16)
        if column_moves:
            sort_rows(place_ref[4], target, outs[:count], column_moves, 0)
            sort_rows(place_ref[4], plane_target, outs[count:], plane_moves, 0)

    whole = [((width, columns), BF16), ((rank_width, width), BF16)]
    if column_moves:
        outs = [((rows_, columns), BF16) for rows_ in out_rows[0]]
        outs += [((rows_, width), BF16) for rows_ in out_rows[1]]
    else:
        outs = whole
    scratch = [pltpu.VMEM(shape, dtype) for shape, dtype in whole] if column_moves else []
    return local_call(
        kernel,
        outs,
        place,
        *normed,
        *grads,
        *context,
        *attended,
        sums,
        rank_sums,
        flops=4 * rows * width * columns + 4 * rows * rank_width * width,
        scratch=scratch + [pltpu.VMEM((extra, width), F32)],
    )


def norm_forward(place, inputs, shares, vectors):
    rows, width = inputs.shape

    def kernel(place_ref, inputs_ref, kept_ref, near_ref, far_ref, vectors_ref, mid_ref, normed_ref):
        for cut in row_chunks(rows):
            attended = kept_ref[cut, :] + near_ref[cut, :].astype(F32)
            attended += far_ref[cut, :].astype(F32)
            mid = inputs_ref[cut, :].astype(F32) + attended + vectors_ref[4:5, :]
            mid_ref[cut, :] = mid
            normed = normalize(mid)[0] * vectors_ref[5:6, :] + vectors_ref[6:7, :]
            normed_ref[cut, :] = normed.astype(BF16)

    return local_call(
        kernel, [((rows, width), F32), ((rows, width), BF16)], place, inputs, *shares, vectors
    )


def norm_grads(place, residual, values, shares, vectors, gain_row, with_sums):
    rows, width = residual.shape

    def kernel(
        place_ref, residual_ref, values_ref, kept_ref, near_ref, far_ref, vectors_ref, *out_refs
    ):
        totals = [jnp.zeros((1, width), F32)] * 3
        for cut in row_chunks(rows):
            grad = kept_ref[cut, :] + near_ref[cut, :].astype(F32)
            grad += far_ref[cut, :].astype(F32)
            normalized, inverse = normalize(values_ref[cut, :].astype(F32))
            gain = vectors_ref[gain_row : gain_row + 1, :]
            result = residual_ref[cut, :] + norm_backward(grad, normalized, inverse, gain)
            out_refs[0][cut, :] = result
            if with_sums:
                rounded = result.astype(BF16)
                out_refs[1][cut, :] = rounded
                terms = (grad * normalized, grad, rounded)
                totals = [total + column_sums(term) for total, term in zip(totals, terms)]
        if with_sums:
            for row, total in enumerate(totals):
                out_refs[2][row : row + 1, :] = total

    outs = [((rows, width), F32)]
    if with_sums:
        outs += [((rows, width), BF16), ((3, width), F32)]
    return local_call(kernel, outs, place, residual, values, *shares, vectors)


class Layout:
    def __init__(self, dp):
        self.dp = dp
        self.count = dp * 2
        self.planes = dp // 4
        self.direct = self.planes == 4
        self.dp_index = lax.axis_index("dp")
        self.core = lax.axis_index("seq")
        self.z = self.dp_index // 4
        self.y = (self.dp_index // 2) % 2
        self.x = self.dp_index % 2
        self.rank = (self.z % 2) * 2 + self.core

    def swap(self, values, mask):
        return swap(values, mask, self.count)

    def gather_tokens(self, values):
        across = self.swap(values, ALONG_Z)
        return (values, self.swap(values, CORE)), (across, self.swap(across, CORE))

    def scatter_tokens(self, own, far):
        crossing = (far[0] + self.swap(far[1], CORE).astype(F32)).astype(BF16)
        return own[0], self.swap(own[1], CORE), self.swap(crossing, ALONG_Z)

    def from_column(self, same, other):
        return (
            self.swap(other, ALONG_Z),
            self.swap(same, ALONG_Z2),
            self.swap(other, ALONG_Z | ALONG_Z2),
        )

    def spread_plane(self, first, second):
        first_x = self.swap(first, ALONG_X)
        second_y = self.swap(second, ALONG_Y)
        first_y = self.swap(jnp.concatenate([first, first_x]), ALONG_Y)
        second_x = self.swap(jnp.concatenate([second, second_y]), ALONG_X)
        return [first, first_x, first_y, second, second_y, second_x]

    def gather_columns(self, same, other, extra):
        rows, columns = same.shape
        if not self.direct:
            whole = self.gather_columns_plainly(same, other)
            return whole, whole[:, columns - extra :].astype(F32).T
        by_1, by_2, by_3 = self.from_column(same, other)
        spread = self.spread_plane(jnp.concatenate([same, by_2]), jnp.concatenate([by_1, by_3]))
        return move_blocks(
            spread, self.column_moves(rows, 2 * rows, 0), [self.dp * rows], self.dp_index, extra
        )

    def gather_columns_plainly(self, same, other):
        low = self.rank < 2
        both = jnp.stack([jnp.where(low, same, other), jnp.where(low, other, same)])
        whole = lax.all_gather(both, "dp", axis=0)
        mine = lax.dynamic_index_in_dim(whole, self.rank // 2, 1, keepdims=False)
        return mine.reshape(-1, same.shape[1])

    def column_moves(self, rows, stride, out):
        moves = []
        for far_z in range(2):
            first = far_z * rows
            for array, row, flip in (
                (0, first, 0),
                (1, first, 1),
                (2, first, 2),
                (2, stride + first, 3),
                (3, first, 4),
                (4, first, 6),
                (5, first, 5),
                (5, stride + first, 7),
            ):
                moves.append((array, always(row), out, xor_row(flip + 8 * far_z, rows), rows))
        return moves

    def gather_plane_rows(self, shard):
        rows, columns = shard.shape
        if not self.direct:
            whole = lax.all_gather(shard, "dp", axis=0, tiled=True)
            quarter = self.dp * rows // RANKS
            return lax.dynamic_slice_in_dim(whole, self.rank * quarter, quarter, 0)
        mine = lax.ppermute(shard, AXES, plane_route(self.planes))
        by_x = self.swap(mine, ALONG_X)
        by_y = self.swap(jnp.concatenate([mine, by_x]), ALONG_Y)
        sources = ((0, 0, 0), (1, 0, 1), (2, 0, 2), (2, rows, 3))
        moves = [
            (array, always(row), 0, xor_row(flip, rows, 0, 3), rows) for array, row, flip in sources
        ]
        return move_blocks([mine, by_x, by_y], moves, [4 * rows], self.dp_index)[0]

    def feed_forward_blocks(self, w_up, w_down):
        shard, hidden = w_up.shape
        columns = hidden // RANKS
        same = lax.dynamic_slice_in_dim(w_up, self.rank * columns, columns, 1)
        other = lax.dynamic_slice_in_dim(w_up, (self.rank ^ 2) * columns, columns, 1)
        if not self.direct:
            return same, other
        by_1, by_2, by_3 = self.from_column(same, other)
        mine = lax.ppermute(w_down, AXES, plane_route(self.planes))
        half = w_down.shape[0] // 2
        return (
            jnp.concatenate([same, by_2, mine[:half]]),
            jnp.concatenate([by_1, by_3, mine[half:]]),
        )

    def place_feed_forward(self, arrays, shard, rows):
        half = rows // 2
        moves = []
        for flip in range(4):
            for odd in range(2):
                array = 4 * odd + flip
                for far_z in range(2):
                    target = xor_row(flip + 4 * (odd + 2 * far_z), shard)
                    moves.append((array, always(far_z * shard), 0, target, shard))
                target = xor_row(flip, rows, odd * half, 3)
                moves.append((array, always(2 * shard), 1, target, half))
        return move_blocks(arrays, moves, [self.dp * shard, 4 * rows], self.dp_index)

    def sum_first(self, kept, received):
        both = kept.astype(F32) + received.astype(F32)
        rows = both.shape[0] // 2
        return both[:rows], both[rows:].astype(BF16)

    def both_cores(self, first, second, rows):
        blocks = jnp.stack([first[:rows], second[:rows], first[rows : 2 * rows], second[rows : 2 * rows]])
        blocks = blocks.reshape(4, 2, rows // 2, first.shape[1])
        mine = lax.dynamic_index_in_dim(blocks, self.core, 1, keepdims=False)
        away = lax.dynamic_index_in_dim(blocks, 1 - self.core, 1, keepdims=False).astype(BF16)
        return jnp.stack([mine.astype(BF16), self.swap(away, CORE)], axis=1)

    def from_column_chips(self, both):
        return [self.swap(both[step], step * ALONG_Z) for step in range(1, 4)]

    def sum_column(self, both, by):
        near = both[0].astype(F32) + by[1].astype(F32)
        far = by[0].astype(F32) + by[2].astype(F32)
        return self.in_rank_order([near[0], near[1], far[0], far[1]])

    def in_rank_order(self, ranks):
        high, low = self.rank // 2 == 1, self.rank % 2 == 1
        ranks = [jnp.where(low, ranks[i ^ 1], ranks[i]) for i in range(4)]
        return [jnp.where(high, ranks[i ^ 2], ranks[i]) for i in range(4)]

    def column_parts(self, rows, extra, array):
        moves = []
        half = 2 * rows + extra
        for out, flips in enumerate(((0, 1), (2, 3), (4, 6), (5, 7))):
            for block, flip in enumerate(flips):
                for far_z in range(2):
                    target = block * half + far_z * rows
                    moves.append(
                        (array, xor_row(flip + 8 * far_z, rows), out, always(target), rows)
                    )
        return moves

    def column_order(self, rows):
        return (self.column_parts(rows, 0, 0), [4 * rows] * 4) if self.direct else ([], [])

    def scatter_columns_plainly(self, grads):
        dp, rows, columns = self.dp, grads.shape[0] // self.dp, grads.shape[1]
        whole = jnp.zeros((dp * rows, RANKS, columns), BF16)
        whole = lax.dynamic_update_slice_in_dim(whole, grads[:, None, :], self.rank, 1)
        mine = lax.psum_scatter(
            whole.reshape(dp * rows, RANKS * columns).astype(F32),
            AXES,
            scatter_dimension=0,
            tiled=True,
        )
        return [mine[:, rank * columns : (rank + 1) * columns] for rank in range(RANKS)]

    def plane_order(self, rows):
        if not self.direct:
            return [], []
        moves = [
            (0, xor_row(flip, rows, 0, 3), flip // 2, always(flip % 2 * rows), rows)
            for flip in range(4)
        ]
        return moves, [2 * rows] * 2

    def scatter_plane_rows_plainly(self, grads):
        rows, columns = grads.shape
        whole = jnp.zeros((RANKS, rows, columns), BF16)
        whole = lax.dynamic_update_slice_in_dim(whole, grads[None], self.rank, 0)
        return lax.psum_scatter(
            whole.reshape(RANKS * rows, columns).astype(F32),
            AXES,
            scatter_dimension=0,
            tiled=True,
        )

    def to_owners(self, lower, upper):
        back = [(target, source) for source, target in plane_route(self.planes)]
        crossed = [(source, target ^ CORE) for source, target in back]
        high = self.z // 2 == 1
        straight = jnp.where(high, upper, lower).astype(BF16)
        other = jnp.where(high, lower, upper).astype(BF16)
        return lax.ppermute(straight, AXES, back), lax.ppermute(other, AXES, crossed)

    def feed_forward_order(self, shard, rows):
        if not self.direct:
            return [], []
        half = rows // 2
        stride = 2 * shard + half
        moves = self.column_parts(shard, half, 0)
        for out, (flips, upper) in enumerate((((0, 1), 0), ((2, 3), 0), ((0, 2), 1), ((1, 3), 1))):
            for block, flip in enumerate(flips):
                target = always(block * stride + 2 * shard)
                moves.append((1, xor_row(flip, rows, upper * half, 3), out, target, half))
        return moves, [2 * stride] * 4


def on_device(
    dp,
    inputs,
    lengths,
    cotangent,
    norm1_gain,
    norm1_shift,
    w_query,
    b_query,
    w_key,
    w_value,
    b_value,
    w_output,
    b_output,
    norm2_gain,
    norm2_shift,
    w_up,
    b_up,
    w_down,
    b_down,
):
    at = Layout(dp)
    tokens, width = inputs.shape
    shard = w_query.shape[0]
    hidden_width = w_up.shape[1]
    rank_width = width // RANKS
    rank_hidden = hidden_width // RANKS

    partner_length = at.swap(lengths, ALONG_Z)
    place = jnp.stack([at.core, at.rank, lengths[0], partner_length[0], at.dp_index])
    place = place.astype(jnp.int32)
    here = jnp.stack([at.core, at.rank]).astype(jnp.int32)

    vectors = [norm1_gain, norm1_shift, b_query, b_value, b_output, norm2_gain, norm2_shift, b_down]
    extra = len(vectors) + b_up.shape[0] // shard
    same, other = cut_projections(here, (w_query, w_key, w_value), (*vectors, b_up))
    own_inputs, far_inputs = at.gather_tokens(inputs)
    qkv, vectors = at.gather_columns(same, other, extra)
    up_bias = vectors[8:].reshape(extra - 8, dp, shard).transpose(1, 0, 2).reshape(1, hidden_width)
    up_bias = lax.dynamic_slice_in_dim(up_bias, at.rank * rank_hidden, rank_hidden, 1)
    out_rows = at.gather_plane_rows(w_output)

    positions = at.core * tokens + jnp.arange(tokens, dtype=jnp.int32)
    own_valid = (positions < lengths[0]).astype(F32)[:, None]
    grad_out = cotangent.astype(F32) * own_valid
    grad_branch = grad_out.astype(BF16)
    branch_across = at.swap(grad_branch, ALONG_Z)
    first, second = at.feed_forward_blocks(w_up, w_down)
    to_x = lambda values: at.swap(values, ALONG_X)
    to_y = lambda values: at.swap(values, ALONG_Y)

    far_clip = attention_forward(place, 1, far_inputs, qkv, vectors, out_rows)
    if at.direct:
        far_clip, first_x, second_y, branch_across = together(
            far_clip, to_x(first), to_y(second), branch_across
        )
    crossing = (far_clip[3] + at.swap(far_clip[4], CORE).astype(F32)).astype(BF16)
    far_share = at.swap(crossing, ALONG_Z)
    own_clip = attention_forward(place, 0, tie(own_inputs, crossing), qkv, vectors, out_rows)
    near_share = at.swap(own_clip[4], CORE)
    if at.direct:
        own_clip, far_share, first_y, second_x = together(
            own_clip, far_share, to_y(first), to_x(second)
        )
    mid, normed2 = norm_forward(place, inputs, (own_clip[3], near_share, far_share), vectors)

    far_normed2 = at.swap(normed2, ALONG_Z)
    own_normed2 = (normed2, at.swap(normed2, CORE))
    if at.direct:
        far_normed2, first_xy, second_yx = together(far_normed2, to_y(first_x), to_x(second_y))
        arrays = [first, first_x, first_y, first_xy, second, second_x, second_y, second_yx]
        up, down = at.place_feed_forward(arrays, shard, w_down.shape[0])
    else:
        up, down = at.gather_columns_plainly(first, second), at.gather_plane_rows(w_down)
    early = tie(grad_branch, mid)
    own_branch = (grad_branch, at.swap(early, CORE))
    branch_across = tie(branch_across, mid)
    far_branch = (branch_across, at.swap(branch_across, CORE))
    far_normed2 = (far_normed2, at.swap(far_normed2, CORE))

    own = feed_forward(place, own_normed2, own_branch, up, down, up_bias)
    far = feed_forward(place, far_normed2, far_branch, up, down, up_bias)
    shares = at.scatter_tokens(own[3:], far[3:])
    grad_mid, grad_attended, norm2_sums = norm_grads(
        place, grad_out, mid, shares, vectors, 5, True
    )
    moves, sizes = at.feed_forward_order(shard, hidden_width // dp)
    sorted_grads = feed_forward_grads(
        place,
        (own[0], far[0]),
        (own[1], far[1]),
        own_normed2 + far_normed2,
        own_branch + far_branch,
        moves,
        sizes,
    )
    own_out, far_out = feed_forward_out(place, tie(own[0], far[4]), down), feed_forward_out(place, far[0], down)
    out_near = at.swap(own_out[1], CORE)
    out_crossing = (far_out[0] + at.swap(far_out[1], CORE).astype(F32)).astype(BF16)

    across = at.swap(grad_attended, ALONG_Z)
    own_attended = (grad_attended, at.swap(grad_attended, CORE))
    own_back = attention_backward(
        place, 0, own_attended, own_inputs, own_clip[1], qkv, vectors, out_rows
    )
    across = tie(across, own_back[2])
    far_attended = (across, at.swap(across, CORE))
    out_far = at.swap(tie(out_crossing, across), ALONG_Z)
    far_back = attention_backward(
        place, 1, far_attended, far_inputs, far_clip[1], qkv, vectors, out_rows
    )

    if at.direct:
        kept_1, sent_1, kept_2, sent_2 = sorted_grads
        up_first = at.sum_first(tie(kept_1, own_back[2]), at.swap(sent_1, ALONG_Y))
        up_second = at.sum_first(tie(kept_2, own_back[2]), at.swap(sent_2, ALONG_X))
        up_received = at.swap(up_first[1], ALONG_X), at.swap(up_second[1], ALONG_Y)
    else:
        grad_w_up = at.scatter_columns_plainly(sorted_grads[0])
        grad_w_down = at.scatter_plane_rows_plainly(sorted_grads[1])

    norm1_sums = own_back[3] + far_back[3]
    head_sums = own_back[4] + far_back[4]
    up_sums = (own[2] + far[2]).reshape(2 * dp // RANKS, extra - 8, shard // 2)
    up_sums = up_sums.transpose(1, 0, 2).reshape(extra - 8, rank_width)
    branch_sums = column_sums(grad_branch)
    nothing = jnp.zeros((2, width), F32)
    sums = jnp.concatenate(
        [norm1_sums, nothing, norm2_sums[2:], norm2_sums[:2], branch_sums, nothing, nothing]
    )
    nothing = jnp.zeros((4, rank_width), F32)
    rank_sums = jnp.concatenate(
        [
            nothing[:2],
            head_sums[:, :rank_width],
            head_sums[:, 2 * rank_width :],
            nothing,
            up_sums,
        ]
    )
    column_moves, column_sizes = at.column_order(shard)
    plane_moves, plane_sizes = at.plane_order(shard)
    sorted_grads = attention_grads(
        place,
        (own_clip[0], far_clip[0]),
        (own_back[0], far_back[0]),
        (own_clip[2], far_clip[2]),
        own_attended + far_attended,
        sums,
        rank_sums,
        (column_moves, plane_moves),
        (column_sizes, plane_sizes),
    )
    back_near = at.swap(own_back[2], CORE)
    back_crossing = (far_back[1] + at.swap(far_back[2], CORE).astype(F32)).astype(BF16)
    if at.direct:
        half = shard // 2
        *sorted_grads, out_far, back_far, received_1, received_2 = together(
            *sorted_grads, out_far, at.swap(back_crossing, ALONG_Z), *up_received
        )
        kept_1, sent_1, kept_2, sent_2, output_kept, output_sent = sorted_grads
        first, second = up_first[0] + received_1.astype(F32), up_second[0] + received_2.astype(F32)
        up_both = at.both_cores(first, second, shard)
        received_1, received_2, output_sent, up_both, *owners = together(
            at.swap(sent_1, ALONG_Y),
            at.swap(sent_2, ALONG_X),
            at.swap(output_sent, ALONG_Y),
            up_both,
            *at.to_owners(first[2 * shard :], second[2 * shard :]),
        )
        qkv_first, qkv_second = at.sum_first(kept_1, received_1), at.sum_first(kept_2, received_2)
        received_1, received_2, *up_by = together(
            at.swap(qkv_first[1], ALONG_X),
            at.swap(qkv_second[1], ALONG_Y),
            *at.from_column_chips(up_both),
        )
        grad_w_down = owners[0].astype(F32) + owners[1].astype(F32)
        grad_w_up = at.sum_column(up_both, up_by)
        first = qkv_first[0] + received_1.astype(F32)
        second = qkv_second[0] + received_2.astype(F32)
        output_first = at.sum_first(output_kept, output_sent)
        grad_output = output_first[0] + at.swap(output_first[1], ALONG_X).astype(F32)
        both = at.both_cores(first, second, shard)
        by = at.from_column_chips(both)
        *by, lower, upper = together(*by, *at.to_owners(grad_output[:half], grad_output[half:]))
        by_rank = at.sum_column(both, by)
        grad_w_output = lower.astype(F32) + upper.astype(F32)
    else:
        back_far = at.swap(back_crossing, ALONG_Z)
        by_rank = at.scatter_columns_plainly(sorted_grads[0])
        grad_w_output = at.scatter_plane_rows_plainly(sorted_grads[1])
    shares = (own_back[1], back_near, back_far)
    (input_grad,) = norm_grads(place, grad_mid, inputs, shares, vectors, 0, False)
    grad_w_up = jnp.concatenate(grad_w_up, axis=1)
    branch = own_out[0] + out_near.astype(F32) + out_far.astype(F32)
    output = (mid + branch + vectors[7:8]).astype(BF16)
    grad_w_query, grad_w_key, grad_w_value = (
        jnp.concatenate([part[:, i * rank_width : (i + 1) * rank_width] for part in by_rank], axis=1)
        for i in range(3)
    )
    sums = sum(part[:, 3 * rank_width :] for part in by_rank)
    shares = [sums[:, i] for i in range(8)] + [sums[:, 8:].T.reshape(-1)]
    return (
        output,
        input_grad,
        shares[0],
        shares[1],
        grad_w_query,
        shares[2],
        grad_w_key,
        grad_w_value,
        shares[3],
        grad_w_output,
        shares[4],
        shares[5],
        shares[6],
        grad_w_up,
        shares[8],
        grad_w_down,
        shares[7],
    )


def solution(mesh):
    rows, vector = P("dp", None), P("dp")
    own_rows, own_vector = P(AXES, None), P(AXES)
    return jax.shard_map(
        functools.partial(on_device, mesh.shape["dp"]),
        mesh=mesh,
        in_specs=(
            own_rows,
            vector,
            own_rows,
            vector,
            vector,
            rows,
            vector,
            rows,
            rows,
            vector,
            rows,
            vector,
            vector,
            vector,
            rows,
            vector,
            rows,
            vector,
        ),
        out_specs=(
            own_rows,
            own_rows,
            own_vector,
            own_vector,
            own_rows,
            own_vector,
            own_rows,
            own_rows,
            own_vector,
            own_rows,
            own_vector,
            own_vector,
            own_vector,
            own_rows,
            own_vector,
            own_rows,
            own_vector,
        ),
        check_vma=False,
    )
```
